512 devices in a mesh: grp: 16 (over y_hi, x, core), inner: 32 (over z, y_lo).
Axes of the slice: x: 4, y: 4 (y_hi: 2, y_lo: 2; y = y_hi * 2 + y_lo), z: 16, core: 2. Of those that a mesh axis runs over, the one named last changes fastest.
Arguments:
- tokens: bfloat16 [256, 128, 8, 512], P('grp', 'inner'), may hold values from -6 to 6
- conv_weight: bfloat16 [27, 512], replicated, may hold values from -0.59765625 to 0.59765625
- gain: float32 [512], replicated, may hold values from 0.1 to 1.9
- bands: int32 [4, 2], replicated, may hold values from 0 to 3, as said below
- w_query: bfloat16 [512, 512], replicated, may hold values from -1 to 1
- w_key: bfloat16 [512, 512], replicated, may hold values from -1 to 1
- w_value: bfloat16 [512, 512], replicated, may hold values from -0.25 to 0.25
- w_out: bfloat16 [512, 512], replicated, may hold values from -0.25 to 0.25
- grad_out: bfloat16 [256, 128, 8, 512], P('grp', 'inner'), may hold values from -6 to 6
Outputs:
- output: bfloat16 [256, 128, 8, 512], P('grp', 'inner')
- grad_tokens: bfloat16 [256, 128, 8, 512], P('grp', 'inner')
The draws below stay inside these ranges and needn't reach their ends.
Inputs may be any that keep to these rules, and one draw needn't show every extreme that they name: bands[i, 0] and bands[i, 1] count key blocks of 64 tokens below and above query block i.
All inputs are finite; a program needn't handle non-finite values.
Results may differ from the reference program's by a relative error of at most 0.013.
Values may be sent and summed in bfloat16 or wider, within the bound.
A program may use at most 64 MiB of HBM per device.

```python
import math
import jax
import jax.numpy as jnp
from jax import lax

D = 512
HEADS = 8
HEAD_DIM = 64
WID = 8
DEPTH = 256
HEIGHT = 128
NBLK = 4


def pair_weights(key, share):
    first_key, second_key = jax.random.split(key)
    base = jax.random.normal(first_key, (D, D), jnp.float32) * D ** (-0.5)
    other = jax.random.normal(second_key, (D, D), jnp.float32) * D ** (-0.5)
    partner = share * base + math.sqrt(1.0 - share * share) * other
    return (jnp.clip(base, -1.0, 1.0), jnp.clip(partner, -1.0, 1.0))


def draw_w_query(key, part):
    pair = pair_weights(key, 0.3)
    return pair[0].astype(jnp.bfloat16)


def draw_w_key(key, part):
    pair = pair_weights(key, 0.3)
    return pair[1].astype(jnp.bfloat16)


def draw_tokens(key, part):
    key = jax.random.fold_in(key, 11)
    shape = (DEPTH, HEIGHT, WID, D)
    result = jnp.clip(jax.random.normal(key, shape, jnp.float32), -6.0, 6.0)
    return result.astype(jnp.bfloat16)


def draw_bands(key, part):
    key = jax.random.fold_in(key, 23)
    values = jax.random.randint(key, (NBLK, 2), 0, NBLK)
    values = values.at[NBLK - 1, 0].set(0)
    values = values.at[0, 1].set(NBLK - 1)
    return values.astype(jnp.int32)


def block_levels(own_key, dims, shards, low, top_value):
    def one(axis_at, parts):
        heights = jax.random.uniform(jax.random.fold_in(jax.random.fold_in(own_key, 6), axis_at), (parts,), jnp.float32, low / len(shards), top_value / len(shards))
        return jnp.repeat(jnp.exp(heights), dims[axis_at] // parts).reshape((-1,) + (1,) * (len(dims) - axis_at - 1))

    factor_of = one(*shards[0])
    for cut in shards[1:]:
        factor_of = factor_of * one(*cut)
    return factor_of


def noise(stream_key, dims, spread, reach, cuts=(), held_as=jnp.bfloat16):
    values = spread * jax.random.normal(stream_key, dims, jnp.float32)
    if cuts:
        values = values * block_levels(stream_key, dims, cuts, -0.22, 0.18)
    return jnp.clip(values, -reach, reach).astype(held_as)


def setup_inputs(seed: int = 0) -> dict:
    key_of = jax.random.split(jax.random.key(seed), 10)
    tokens = draw_tokens(jax.random.fold_in(key_of[9], 71), 0)
    conv_weight = noise(key_of[1], (27, D), 0.1, 0.59765625)
    gain = jnp.clip(1.0 + 0.18 * jax.random.normal(key_of[2], (D,), jnp.float32), 0.1, 1.9)
    bands = draw_bands(jax.random.fold_in(key_of[9], 71), 0)
    w_query = draw_w_query(jax.random.fold_in(key_of[9], 71), 0)
    w_key = draw_w_key(jax.random.fold_in(key_of[9], 71), 0)
    w_value = noise(key_of[6], (D, D), D ** -0.5, 0.25)
    w_out = noise(key_of[7], (D, D), D ** -0.5, 0.25)
    grad_out = noise(key_of[8], (DEPTH, HEIGHT, WID, D), 1.0, 6.0, ((0, 16), (1, 32)))
    return dict(tokens=tokens, conv_weight=conv_weight, gain=gain, bands=bands, w_query=w_query, w_key=w_key, w_value=w_value, w_out=w_out, grad_out=grad_out)


def conv_forward(padded, taps):
    dep = padded.shape[0] - 2
    hgt = padded.shape[1] - 2
    wid = padded.shape[2] - 2
    total = jnp.zeros((dep, hgt, wid, padded.shape[3]), jnp.float32)
    for first in range(3):
        for second in range(3):
            for third in range(3):
                tap = taps[first * 9 + second * 3 + third]
                total = total + tap * padded[first:first + dep, second:second + hgt, third:third + wid].astype(jnp.float32)
    return total

def conv_adjoint(padded, taps):
    dep = padded.shape[0] - 2
    hgt = padded.shape[1] - 2
    wid = padded.shape[2] - 2
    total = jnp.zeros((dep, hgt, wid, padded.shape[3]), jnp.float32)
    for first in range(3):
        for second in range(3):
            for third in range(3):
                tap = taps[first * 9 + second * 3 + third]
                total = total + tap * padded[2 - first:2 - first + dep, 2 - second:2 - second + hgt, 2 - third:2 - third + wid].astype(jnp.float32)
    return total

def layer_norm(filtered, gain):
    values = filtered.astype(jnp.float32)
    centred = values - lax.optimization_barrier(jnp.mean(values, -1, keepdims=True))
    scale = lax.rsqrt(lax.optimization_barrier(jnp.mean(centred * centred, -1, keepdims=True)) + 1e-05)
    return centred * scale * gain

def layer_norm_back(filtered, gain, grad_normed):
    values = filtered.astype(jnp.float32)
    centred = values - lax.optimization_barrier(jnp.mean(values, -1, keepdims=True))
    scale = lax.rsqrt(lax.optimization_barrier(jnp.mean(centred * centred, -1, keepdims=True)) + 1e-05)
    unit = centred * scale
    scaled = grad_normed.astype(jnp.float32) * gain
    return scale * (scaled - lax.optimization_barrier(jnp.mean(scaled, -1, keepdims=True)) - unit * lax.optimization_barrier(jnp.mean(scaled * unit, -1, keepdims=True)))

def band_mask(bands, length):
    blocks = bands.shape[0]
    block_len = length // blocks
    query_block = jnp.arange(length, dtype=jnp.int32) // block_len
    onehot = (query_block[:, None] == jnp.arange(blocks, dtype=jnp.int32)[None, :]).astype(jnp.int32)
    lower = lax.optimization_barrier(jnp.sum(onehot * bands[None, :, 0], 1))
    upper = lax.optimization_barrier(jnp.sum(onehot * bands[None, :, 1], 1))
    low_edge = (query_block - lower)[:, None]
    high_edge = (query_block + upper)[:, None]
    return (query_block[None, :] >= low_edge) & (query_block[None, :] <= high_edge)

def softmax_probs(query_heads, key_heads, bands):
    length = query_heads.shape[0]
    scores = jnp.einsum('qchd,kchd->chqk', query_heads.astype(jnp.float32), key_heads.astype(jnp.float32)) * (1.0 / math.sqrt(HEAD_DIM))
    allowed = band_mask(bands, length)
    masked = jnp.where(allowed, scores, -1e+30)
    top = lax.optimization_barrier(jnp.max(masked, -1, keepdims=True))
    expo = jnp.where(allowed, jnp.exp(masked - top), 0.0)
    return expo / lax.optimization_barrier(jnp.sum(expo, -1, keepdims=True))

def attend(query, keys, values, bands):
    length, cols = (query.shape[0], query.shape[1])
    shape = (length, cols, HEADS, HEAD_DIM)
    query_heads, key_heads, value_heads = (query.reshape(shape), keys.reshape(shape), values.reshape(shape))
    weights = softmax_probs(query_heads, key_heads, bands).astype(jnp.bfloat16)
    result = jnp.einsum('chqk,kchd->qchd', weights.astype(jnp.float32), value_heads.astype(jnp.float32))
    return result.astype(jnp.bfloat16).reshape(length, cols, HEADS * HEAD_DIM)

def attend_back(query, keys, values, grad_att, bands):
    length, cols = (query.shape[0], query.shape[1])
    shape = (length, cols, HEADS, HEAD_DIM)
    query_heads, key_heads, value_heads = (query.reshape(shape), keys.reshape(shape), values.reshape(shape))
    grad_heads = grad_att.reshape(shape)
    probs = softmax_probs(query_heads, key_heads, bands)
    weights = probs.astype(jnp.bfloat16)
    grad_probs = jnp.einsum('qchd,kchd->chqk', grad_heads.astype(jnp.float32), value_heads.astype(jnp.float32))
    grad_value = jnp.einsum('chqk,qchd->kchd', weights.astype(jnp.float32), grad_heads.astype(jnp.float32)).astype(jnp.bfloat16)
    centre = lax.optimization_barrier(jnp.sum(probs * grad_probs, -1, keepdims=True))
    grad_scores = (probs * (grad_probs - centre) * (1.0 / math.sqrt(HEAD_DIM))).astype(jnp.bfloat16)
    grad_query = jnp.einsum('chqk,kchd->qchd', grad_scores.astype(jnp.float32), key_heads.astype(jnp.float32)).astype(jnp.bfloat16)
    grad_key = jnp.einsum('chqk,qchd->kchd', grad_scores.astype(jnp.float32), query_heads.astype(jnp.float32)).astype(jnp.bfloat16)
    flat = (length, cols, HEADS * HEAD_DIM)
    return (grad_query.reshape(flat), grad_key.reshape(flat), grad_value.reshape(flat))

def reference(tokens, conv_weight, gain, bands, w_query, w_key, w_value, w_out, grad_out):
    taps = conv_weight.astype(jnp.float32)
    spacing = ((1, 1), (1, 1), (1, 1), (0, 0))
    filtered = (tokens.astype(jnp.float32) + conv_forward(jnp.pad(tokens, spacing), taps)).astype(jnp.bfloat16)
    normed = layer_norm(filtered, gain).astype(jnp.bfloat16)
    ncol = HEIGHT * WID
    group = math.gcd(ncol, 8)
    flat = normed.reshape(DEPTH, ncol, D)
    w_joint = jnp.concatenate([w_query, w_key, w_value], 1)
    joint = jnp.dot(flat, w_joint, preferred_element_type=jnp.float32).astype(jnp.bfloat16)
    query, keys, values = (joint[:, :, :D], joint[:, :, D:2 * D], joint[:, :, 2 * D:])

    def blocks(array):
        return array.reshape(DEPTH, ncol // group, group, D).transpose(1, 0, 2, 3)

    def unblocks(array):
        return array.transpose(1, 0, 2, 3).reshape(DEPTH, ncol, D)
    attended = unblocks(lax.map(lambda part: attend(part[0], part[1], part[2], bands), (blocks(query), blocks(keys), blocks(values))))
    filtered_flat = filtered.reshape(DEPTH, ncol, D).astype(jnp.float32)
    output = (filtered_flat + jnp.dot(attended, w_out, preferred_element_type=jnp.float32)).astype(jnp.bfloat16)
    grad_flat = grad_out.reshape(DEPTH, ncol, D)
    grad_att = jnp.dot(grad_flat, w_out.T, preferred_element_type=jnp.float32).astype(jnp.bfloat16)
    grads = lax.map(lambda part: attend_back(part[0], part[1], part[2], part[3], bands), (blocks(query), blocks(keys), blocks(values), blocks(grad_att)))
    joined = jnp.concatenate([unblocks(grads[0]), unblocks(grads[1]), unblocks(grads[2])], -1)
    grad_normed = jnp.dot(joined, w_joint.T, preferred_element_type=jnp.float32).astype(jnp.bfloat16)
    grad_normed = grad_normed.reshape(DEPTH, HEIGHT, WID, D)
    grad_filtered = (grad_out.astype(jnp.float32) + layer_norm_back(filtered, gain, grad_normed)).astype(jnp.bfloat16)
    grad_tokens = (grad_filtered.astype(jnp.float32) + conv_adjoint(jnp.pad(grad_filtered, spacing), taps)).astype(jnp.bfloat16)
    return (output.reshape(DEPTH, HEIGHT, WID, D), grad_tokens)
```

```python
import jax
import jax.numpy as jnp
from jax import lax
from jax.experimental import pallas as pl
from jax.experimental.pallas import tpu as pltpu
from jax.sharding import PartitionSpec as P

MESH = pl.DeviceIdType.MESH
F32 = jnp.float32
BF16 = jnp.bfloat16
WID = 512
DEP = 16
HGT = 4
WIN = 8
TOK = DEP * HGT * WIN
COLS = HGT * WIN
LEN = 256
PER = 2


def dot_nn(a, b):
    return lax.dot_general(a, b, (((1,), (0,)), ((), ())), preferred_element_type=F32)


def dot_nt(a, b):
    return lax.dot_general(a, b, (((1,), (1,)), ((), ())), preferred_element_type=F32)


def iota(shape, dim):
    return lax.broadcasted_iota(jnp.int32, shape, dim)


def conv_row(pad, taps, d, h, flip):
    acc = [None, None, None]
    for a in range(3):
        for b in range(3):
            v = pad[d + a, h + b]
            for c in range(3):
                tap = 9 * a + 3 * b + c
                term = taps[26 - tap if flip else tap] * v
                acc[c] = term if acc[c] is None else acc[c] + term
    row = iota((WIN, WID), 0)
    before = jnp.where(row == 0, 0.0, pltpu.roll(acc[0], 1, 0))
    after = jnp.where(row == WIN - 1, 0.0, pltpu.roll(acc[2], WIN - 1, 0))
    return acc[1] + before + after


def kernel(
    bands, conv_w, gain, tok_h, go_h, wq_h, wk_h, wv_h, wo_h, out_ref, gt_ref,
    tok, go, wq, wk, wv, wo, wkt, wvt, taps, pad, edge, rim_d, rim_h, rim_c,
    send_n, send_g, col_n, col_g, send_a, send_b, ret_a, ret_b,
    perm, perm_t, eye, bias, filt, normed, unit, scale,
    q_s, k_s, v_s, g_s, kt_s, vt_s, at_s, qt_s, gk_s, gv_s,
    load_sem, halo_ss, halo_rs, a2a_ss, a2a_rs,
):
    g = lax.axis_index("grp")
    i = lax.axis_index("inner")
    ng = lax.axis_size("grp")
    ni = lax.axis_size("inner")
    up_g, dn_g = lax.rem(g + 1, ng), lax.rem(g + ng - 1, ng)
    up_i, dn_i = lax.rem(i + 1, ni), lax.rem(i + ni - 1, ni)

    loads = []
    for n, (src, dst) in enumerate(
        ((tok_h, tok), (go_h, go), (wq_h, wq), (wk_h, wk), (wv_h, wv), (wo_h, wo))
    ):
        cp = pltpu.make_async_copy(src, dst, load_sem.at[n])
        cp.start()
        loads.append(cp)

    barrier = pltpu.get_barrier_semaphore()
    sides = ((g, up_i), (g, dn_i), (up_g, up_i), (up_g, dn_i), (dn_g, up_i), (dn_g, dn_i))

    def greet(step, carry):
        pl.semaphore_signal(
            barrier, inc=1, device_id=(lax.rem(g + step, ng), i), device_id_type=MESH
        )
        return carry

    lax.fori_loop(1, ng, greet, 0)
    for peer in sides:
        pl.semaphore_signal(barrier, inc=1, device_id=peer, device_id_type=MESH)

    conv_f = conv_w[...].astype(F32)
    for n in range(27):
        taps[n] = jnp.broadcast_to(conv_f[n : n + 1], (WIN, WID))

    loads[0].wait()

    def fill(d, carry):
        pad[1 + d, 1 : 1 + HGT] = (
            tok[pl.ds(d * COLS, COLS)].astype(F32).reshape(HGT, WIN, WID)
        )
        return carry

    def stage(phase):
        for n, h in enumerate((1, HGT)):
            edge[phase, n] = pad[1 : 1 + DEP, h].reshape(DEP * WIN, WID).astype(BF16)

    def halo_copies(phase, body):
        last = DEP * WIN - 16
        plan = (
            (body.at[pl.ds(TOK - COLS, COLS)], rim_d.at[phase, 0], (up_g, i)),
            (body.at[pl.ds(0, COLS)], rim_d.at[phase, 1], (dn_g, i)),
            (edge.at[phase, 1], rim_h.at[phase, 0], (g, up_i)),
            (edge.at[phase, 0], rim_h.at[phase, 1], (g, dn_i)),
            (edge.at[phase, 1, pl.ds(last, 16)], rim_c.at[phase, 0], (up_g, up_i)),
            (edge.at[phase, 1, pl.ds(0, 16)], rim_c.at[phase, 1], (dn_g, up_i)),
            (edge.at[phase, 0, pl.ds(last, 16)], rim_c.at[phase, 2], (up_g, dn_i)),
            (edge.at[phase, 0, pl.ds(0, 16)], rim_c.at[phase, 3], (dn_g, dn_i)),
        )
        return [
            pltpu.make_async_remote_copy(
                src_ref=src, dst_ref=dst, send_sem=halo_ss.at[phase, n],
                recv_sem=halo_rs.at[phase, n], device_id=dev, device_id_type=MESH,
            )
            for n, (src, dst, dev) in enumerate(plan)
        ]

    def rim_in(phase):
        lo_g, hi_g = g > 0, g < ng - 1
        lo_i, hi_i = i > 0, i < ni - 1

        def part(ok, val):
            return jnp.where(ok, val.astype(F32), 0.0)

        pad[0, 1 : 1 + HGT] = part(lo_g, rim_d[phase, 0]).reshape(HGT, WIN, WID)
        pad[DEP + 1, 1 : 1 + HGT] = part(hi_g, rim_d[phase, 1]).reshape(HGT, WIN, WID)
        pad[1 : 1 + DEP, 0] = part(lo_i, rim_h[phase, 0]).reshape(DEP, WIN, WID)
        pad[1 : 1 + DEP, HGT + 1] = part(hi_i, rim_h[phase, 1]).reshape(DEP, WIN, WID)
        pad[0, 0] = part(lo_g & lo_i, rim_c[phase, 0])[WIN:]
        pad[DEP + 1, 0] = part(hi_g & lo_i, rim_c[phase, 1])[:WIN]
        pad[0, HGT + 1] = part(lo_g & hi_i, rim_c[phase, 2])[WIN:]
        pad[DEP + 1, HGT + 1] = part(hi_g & hi_i, rim_c[phase, 3])[:WIN]

    def own_rows(owner):
        return pl.ds(pl.multiple_of(owner * DEP, DEP), DEP)

    def exchange(kind, col, src, dst):
        def one(step, carry):
            p = lax.rem(g + step, ng)
            pltpu.make_async_remote_copy(
                src_ref=src.at[col, own_rows(p)], dst_ref=dst.at[col, own_rows(g)],
                send_sem=a2a_ss.at[kind, col], recv_sem=a2a_rs.at[kind, col],
                device_id=(p, i), device_id_type=MESH,
            ).start()
            return carry

        lax.fori_loop(1, ng, one, 0)
        pltpu.make_async_copy(
            src.at[col, own_rows(g)], dst.at[col, own_rows(g)], a2a_rs.at[kind, col]
        ).start()

    def arrived(kind, col, dst):
        pltpu.make_async_copy(dst.at[col], dst.at[col], a2a_rs.at[kind, col]).wait()

    def sent(kind, col, src):
        rows = pl.ds(0, LEN - DEP)
        pltpu.make_async_copy(
            src.at[col, rows], src.at[col, rows], a2a_ss.at[kind, col]
        ).wait()

    lax.fori_loop(0, DEP, fill, 0)
    stage(0)
    pl.semaphore_wait(barrier, ng - 1 + len(sides))
    halos = halo_copies(0, tok)
    for cp in halos:
        cp.start()

    shape = (TOK, TOK)

    def token_of(s):
        return (s & 15) * COLS + ((s >> 4) & 15) * PER + (s >> 8)

    perm[...] = jnp.where(iota(shape, 1) == token_of(iota(shape, 0)), 1.0, 0.0).astype(BF16)
    perm_t[...] = jnp.where(iota(shape, 0) == token_of(iota(shape, 1)), 1.0, 0.0).astype(BF16)
    eye[...] = jnp.where(iota(shape, 0) == iota(shape, 1), 1.0, 0.0).astype(BF16)

    loads[1].wait()
    for col in range(PER):
        send_g[col] = dot_nn(perm[col * LEN : (col + 1) * LEN], go[...]).astype(BF16)
        exchange(0, col, send_g, col_g)

    for cp in loads[2:]:
        cp.wait()
    wkt[...] = dot_nt(eye[...], wk[...]).astype(BF16)
    wvt[...] = dot_nt(eye[...], wv[...]).astype(BF16)

    square = (LEN, LEN)
    key_block = iota(square, 0) >> 6
    query_block = iota(square, 1) >> 6
    lower = jnp.zeros(square, jnp.int32)
    upper = jnp.zeros(square, jnp.int32)
    for n in range(4):
        lower = jnp.where(query_block == n, bands[n, 0], lower)
        upper = jnp.where(query_block == n, bands[n, 1], upper)
    allowed = (key_block >= query_block - lower) & (key_block <= query_block + upper)
    bias[...] = jnp.where(allowed, 0.0, -1e30)

    for cp in halos:
        cp.wait()
    rim_in(0)

    gain_row = gain[...]

    def forward(d, carry):
        rows = pl.ds(pl.multiple_of(d * COLS, COLS), COLS)
        conv = [
            conv_row(pad, taps, d, h, False) + pad[d + 1, h + 1] for h in range(HGT)
        ]
        vals = jnp.concatenate(conv, 0).astype(BF16)
        filt[rows] = vals
        vals = vals.astype(F32)
        centred = vals - jnp.sum(vals, -1, keepdims=True) * (1.0 / WID)
        var = jnp.sum(centred * centred, -1, keepdims=True) * (1.0 / WID)
        inv = lax.rsqrt(var + 1e-05)
        xhat = centred * inv
        unit[rows] = xhat
        scale[rows] = jnp.broadcast_to(inv, (COLS, 128))
        normed[rows] = (xhat * gain_row).astype(BF16)
        return carry

    lax.fori_loop(0, DEP, forward, 0)
    for col in range(PER):
        send_n[col] = dot_nn(perm[col * LEN : (col + 1) * LEN], normed[...]).astype(BF16)
        exchange(1, col, send_n, col_n)

    low_half = iota((LEN, 128), 1) < 64

    def halves(x):
        zero = jnp.zeros_like(x)
        return jnp.where(low_half, x, zero), jnp.where(low_half, zero, x)

    for col in range(PER):
        arrived(0, col, col_g)
        g_s[...] = dot_nt(col_g[col], wo[...]).astype(BF16)
        arrived(1, col, col_n)
        x = col_n[col]
        q_s[...] = (dot_nn(x, wq[...]).astype(BF16).astype(F32) * 0.125).astype(BF16)
        k_s[...] = dot_nn(x, wk[...]).astype(BF16)
        v_s[...] = dot_nn(x, wv[...]).astype(BF16)
        kt_s[...] = dot_nt(wkt[...], x).astype(BF16)
        vt_s[...] = dot_nt(wvt[...], x).astype(BF16)

        def heads(pair, carry):
            lanes = pl.ds(pl.multiple_of(pair * 128, 128), 128)
            q2, g2 = q_s[:, lanes], g_s[:, lanes]
            ks, vs = halves(k_s[:, lanes]), halves(v_s[:, lanes])
            qs, gs = halves(q2), halves(g2)
            gk = None
            gv = None
            for n in range(2):
                feats = pl.ds(pl.multiple_of(pair * 128 + n * 64, 64), 64)
                scores = dot_nt(ks[n], q2) + bias[...]
                expo = jnp.exp(scores - jnp.max(scores, 0, keepdims=True))
                probs = expo * (1.0 / jnp.sum(expo, 0, keepdims=True))
                weights = probs.astype(BF16)
                at_s[feats] = dot_nn(vt_s[feats], weights).astype(BF16)
                grad_p = dot_nt(vs[n], g2)
                centre = jnp.sum(probs * grad_p, 0, keepdims=True)
                grad_s = (probs * (grad_p - centre)).astype(BF16)
                qt_s[feats] = (dot_nn(kt_s[feats], grad_s) * 0.125).astype(BF16)
                part_v = dot_nn(weights, gs[n])
                part_k = dot_nn(grad_s, qs[n])
                gv = part_v if gv is None else gv + part_v
                gk = part_k if gk is None else gk + part_k
            gk_s[:, lanes] = gk.astype(BF16)
            gv_s[:, lanes] = gv.astype(BF16)
            return carry

        lax.fori_loop(0, 4, heads, 0)
        small = eye[0:LEN, 0:LEN]
        gq = dot_nt(small, qt_s[...]).astype(BF16)
        send_b[col] = (
            dot_nt(gq, wq[...]) + dot_nt(gk_s[...], wk[...]) + dot_nt(gv_s[...], wv[...])
        ).astype(BF16)
        exchange(2, col, send_b, ret_b)
        send_a[col] = dot_nt(small, at_s[...]).astype(BF16)
        exchange(3, col, send_a, ret_a)

    for col in range(PER):
        arrived(2, col, ret_b)

    normed_grad = [dot_nn(perm_t[:, 0:LEN], ret_b[0]), dot_nn(perm_t[:, LEN:TOK], ret_b[1])]
    unit_grad = (normed_grad[0] + normed_grad[1]) * gain_row
    xhat = unit[...]
    mean = jnp.sum(unit_grad, -1, keepdims=True) * (1.0 / WID)
    along = jnp.sum(unit_grad * xhat, -1, keepdims=True) * (1.0 / WID)
    inv = scale[...][:, 0:1]
    grad_f = (go[...].astype(F32) + inv * (unit_grad - mean - xhat * along)).astype(BF16)
    tok[...] = grad_f

    lax.fori_loop(0, DEP, fill, 0)
    stage(1)
    halos = halo_copies(1, tok)
    for cp in halos:
        cp.start()

    for col in range(PER):
        arrived(3, col, ret_a)
    att = (
        dot_nn(perm_t[:, 0:LEN], ret_a[0]) + dot_nn(perm_t[:, LEN:TOK], ret_a[1])
    ).astype(BF16)
    out_ref[...] = (filt[...].astype(F32) + dot_nn(att, wo[...])).astype(BF16)

    for cp in halos:
        cp.wait()
    rim_in(1)

    def adjoint(d, carry):
        rows = pl.ds(pl.multiple_of(d * COLS, COLS), COLS)
        conv = [conv_row(pad, taps, d, h, True) + pad[d + 1, h + 1] for h in range(HGT)]
        gt_ref[rows] = jnp.concatenate(conv, 0).astype(BF16)
        return carry

    lax.fori_loop(0, DEP, adjoint, 0)
    for kind, src in enumerate((send_g, send_n, send_b, send_a)):
        for col in range(PER):
            sent(kind, col, src)


def body(tokens, conv_weight, gain, bands, w_query, w_key, w_value, w_out, grad_out):
    whole = (TOK, WID)
    pair = (PER, LEN, WID)
    vmem = pl.BlockSpec(memory_space=pltpu.VMEM)
    hbm = pl.BlockSpec(memory_space=pltpu.HBM)
    scratch = [
        pltpu.VMEM(whole, BF16), pltpu.VMEM(whole, BF16),
        *[pltpu.VMEM((WID, WID), BF16) for _ in range(6)],
        pltpu.VMEM((27, WIN, WID), F32),
        pltpu.VMEM((DEP + 2, HGT + 2, WIN, WID), F32),
        pltpu.VMEM((2, 2, DEP * WIN, WID), BF16),
        pltpu.VMEM((2, 2, COLS, WID), BF16),
        pltpu.VMEM((2, 2, DEP * WIN, WID), BF16),
        pltpu.VMEM((2, 4, 16, WID), BF16),
        *[pltpu.VMEM(pair, BF16) for _ in range(8)],
        *[pltpu.VMEM((TOK, TOK), BF16) for _ in range(3)],
        pltpu.VMEM((LEN, LEN), F32),
        pltpu.VMEM(whole, BF16), pltpu.VMEM(whole, BF16),
        pltpu.VMEM(whole, F32),
        pltpu.VMEM((TOK, 128), F32),
        *[pltpu.VMEM((LEN, WID), BF16) for _ in range(4)],
        *[pltpu.VMEM((WID, LEN), BF16) for _ in range(4)],
        *[pltpu.VMEM((LEN, WID), BF16) for _ in range(2)],
        pltpu.SemaphoreType.DMA((6,)),
        pltpu.SemaphoreType.DMA((2, 8)), pltpu.SemaphoreType.DMA((2, 8)),
        pltpu.SemaphoreType.DMA((4, PER)), pltpu.SemaphoreType.DMA((4, PER)),
    ]
    out, grad = pl.pallas_call(
        kernel,
        out_shape=(jax.ShapeDtypeStruct(whole, BF16), jax.ShapeDtypeStruct(whole, BF16)),
        in_specs=[pl.BlockSpec(memory_space=pltpu.SMEM), vmem, vmem] + [hbm] * 6,
        out_specs=(vmem, vmem),
        scratch_shapes=scratch,
        compiler_params=pltpu.CompilerParams(
            collective_id=0, has_side_effects=True, vmem_limit_bytes=48 * 2**20
        ),
        name="sublayer",
    )(
        bands, conv_weight, gain.reshape(1, WID), tokens.reshape(whole),
        grad_out.reshape(whole), w_query, w_key, w_value, w_out,
    )
    return out.reshape(tokens.shape), grad.reshape(tokens.shape)


def solution(mesh):
    slab = P("grp", "inner", None, None)
    in_specs = (slab, P(), P(), P(), P(), P(), P(), P(), slab)
    return jax.shard_map(
        body, mesh=mesh, in_specs=in_specs, out_specs=(slab, slab), check_vma=False
    )
```

```python
import jax
import jax.numpy as jnp
from jax import lax
from jax.experimental import pallas as pl
from jax.experimental.pallas import tpu as pltpu
from jax.sharding import PartitionSpec as P

MESH = pl.DeviceIdType.MESH
F32 = jnp.float32
BF16 = jnp.bfloat16
WID = 512
DEP = 16
HGT = 4
WIN = 8
TOK = DEP * HGT * WIN
COLS = HGT * WIN
LEN = 256
PER = 2


def dot_nn(a, b):
    return lax.dot_general(a, b, (((1,), (0,)), ((), ())), preferred_element_type=F32)


def dot_nt(a, b):
    return lax.dot_general(a, b, (((1,), (1,)), ((), ())), preferred_element_type=F32)


def iota(shape, dim):
    return lax.broadcasted_iota(jnp.int32, shape, dim)


def conv_row(pad, taps, d, h, flip):
    acc = [None, None, None]
    for a in range(3):
        for b in range(3):
            v = pad[d + a, h + b]
            for c in range(3):
                tap = 9 * a + 3 * b + c
                term = taps[26 - tap if flip else tap] * v
                acc[c] = term if acc[c] is None else acc[c] + term
    row = iota((WIN, WID), 0)
    before = jnp.where(row == 0, 0.0, pltpu.roll(acc[0], 1, 0))
    after = jnp.where(row == WIN - 1, 0.0, pltpu.roll(acc[2], WIN - 1, 0))
    return acc[1] + before + after


def kernel(
    bands_h, conv_h, gain_h, tok_h, go_h, wq_h, wk_h, wv_h, wo_h, out_h, grad_h,
    bands, conv_w, gain, tok, go, wq, wk, wv, wo, wqt, wkt, wvt, taps, pad, edge,
    rim_d, rim_h, rim_c, send_n, send_g, col_n, col_g, send_a, send_b, ret_a, ret_b,
    swap, eye, bias, hot, filt, normed, unit, scale, grad_f, out, gt,
    k_s, v_s, qt_s, kt_s, vt_s, gt_s, at_s, gq_s, gk_s, gv_s, exp_s, inv_s,
    load_sem, halo_ss, halo_rs, a2a_ss, a2a_rs, store_sem,
):
    g = lax.axis_index("grp")
    i = lax.axis_index("inner")
    ng = lax.axis_size("grp")
    ni = lax.axis_size("inner")
    up_g, dn_g = lax.rem(g + 1, ng), lax.rem(g + ng - 1, ng)
    up_i, dn_i = lax.rem(i + 1, ni), lax.rem(i + ni - 1, ni)

    pairs = (
        (tok_h, tok), (conv_h, conv_w), (go_h, go), (bands_h, bands), (gain_h, gain),
        (wq_h, wq), (wk_h, wk), (wv_h, wv), (wo_h, wo),
    )
    loads = [
        pltpu.make_async_copy(src, dst, load_sem.at[n]) for n, (src, dst) in enumerate(pairs)
    ]
    for cp in loads:
        cp.start()

    barrier = pltpu.get_barrier_semaphore()
    sides = ((g, up_i), (g, dn_i), (up_g, up_i), (up_g, dn_i), (dn_g, up_i), (dn_g, dn_i))

    def greet(step, carry):
        pl.semaphore_signal(
            barrier, inc=1, device_id=(lax.rem(g + step, ng), i), device_id_type=MESH
        )
        return carry

    for peer in sides:
        pl.semaphore_signal(barrier, inc=1, device_id=peer, device_id_type=MESH)
    lax.fori_loop(1, ng, greet, 0)

    last = DEP * WIN - 16

    def halo(phase, k, n, src, dst, dev):
        return pltpu.make_async_remote_copy(
            src_ref=src, dst_ref=dst, send_sem=halo_ss.at[phase, k, n],
            recv_sem=halo_rs.at[phase, k, n], device_id=dev, device_id_type=MESH,
        )

    def halo_depth(phase, body, k):
        return [
            halo(phase, k, 0, body.at[DEP - 1, k], rim_d.at[phase, 0, k], (up_g, i)),
            halo(phase, k, 1, body.at[0, k], rim_d.at[phase, 1, k], (dn_g, i)),
        ]

    def halo_side(phase, k):
        to = up_i if k else dn_i
        side = 1 - k
        return [
            halo(phase, k, 2, edge.at[phase, k], rim_h.at[phase, side], (g, to)),
            halo(
                phase, k, 3, edge.at[phase, k, pl.ds(last, 16)],
                rim_c.at[phase, 0, side], (up_g, to),
            ),
            halo(
                phase, k, 4, edge.at[phase, k, pl.ds(0, 16)],
                rim_c.at[phase, 1, side], (dn_g, to),
            ),
        ]

    def start(copies):
        for cp in copies:
            cp.start()

    def finish(copies):
        for cp in copies:
            cp.wait()

    in_g = (g > 0, g < ng - 1)
    in_i = (i > 0, i < ni - 1)

    def part(ok, val):
        return jnp.where(ok, val.astype(F32), 0.0)

    def rim_depth(phase, k):
        for n in range(2):
            pad[(DEP + 1) * n, 1 + 2 * k : 3 + 2 * k] = part(
                in_g[n], rim_d[phase, n, k]
            ).reshape(2, WIN, WID)

    def rim_side(phase, side):
        h = (HGT + 1) * side
        for n in range(2):
            corner = part(in_g[n] & in_i[side], rim_c[phase, n, side])
            pad[(DEP + 1) * n, h] = corner[:WIN] if n else corner[WIN:]
        pad[1 : 1 + DEP, h] = part(in_i[side], rim_h[phase, side]).reshape(DEP, WIN, WID)

    def own_rows(owner):
        return pl.ds(pl.multiple_of(owner * DEP, DEP), DEP)

    high, chip, core = lax.div(g, 8), lax.rem(lax.div(g, 2), 4), lax.rem(g, 2)
    peers = []
    for step in range(ng - 1):
        far_y, far_x = step < 8, (2, 1, 3, 0)[step // 2 % 4]
        same = 1 - (step + 1) % 2
        p_y = 1 - high if far_y else high
        p_x = lax.rem(chip + far_x, 4) if far_x else chip
        p_c = core if same else 1 - core
        peers.append(p_y * 8 + p_x * 2 + p_c)

    def exchange(kind, col, src, dst):
        for p in peers:
            pltpu.make_async_remote_copy(
                src_ref=src.at[col, own_rows(p)], dst_ref=dst.at[col, own_rows(g)],
                send_sem=a2a_ss.at[kind, col], recv_sem=a2a_rs.at[kind, col],
                device_id=(p, i), device_id_type=MESH,
            ).start()
        pltpu.make_async_copy(
            src.at[col, own_rows(g)], dst.at[col, own_rows(g)], a2a_rs.at[kind, col]
        ).start()

    def arrived(kind, col, dst):
        pltpu.make_async_copy(dst.at[col], dst.at[col], a2a_rs.at[kind, col]).wait()

    def sent(kind, col, src):
        rows = pl.ds(0, LEN - DEP)
        pltpu.make_async_copy(
            src.at[col, rows], src.at[col, rows], a2a_ss.at[kind, col]
        ).wait()

    loads[0].wait()

    def fill(d, carry):
        pad[1 + d, 1 : 1 + HGT] = tok[d].reshape(COLS, WID).astype(F32).reshape(HGT, WIN, WID)
        return carry

    lax.fori_loop(0, DEP, fill, 0)
    for k in range(2):
        edge[0, k] = pad[1 : 1 + DEP, 1 + 3 * k].reshape(DEP * WIN, WID).astype(BF16)
    pl.semaphore_wait(barrier, ng - 1 + len(sides))
    depth = halo_depth(0, tok, 0) + halo_depth(0, tok, 1)
    low, top = halo_side(0, 1), halo_side(0, 0)
    start(depth + low + top)

    square = (LEN, LEN)
    row, lane = iota(square, 0), iota(square, 1)
    swap[...] = jnp.where(lane == (row & 15) * 16 + (row >> 4), 1.0, 0.0).astype(BF16)
    eye[...] = jnp.where(row == lane, 1.0, 0.0).astype(BF16)

    loads[2].wait()
    for k in range(2):
        send_g[k] = dot_nn(swap[...], go[:, k].reshape(LEN, WID)).astype(BF16)
    exchange(0, 0, send_g, col_g)

    loads[1].wait()
    conv_f = conv_w[...].astype(F32)
    for n in range(27):
        taps[n] = jnp.broadcast_to(conv_f[n : n + 1], (WIN, WID))

    loads[3].wait()
    slim = (64, LEN)
    key_block = iota(slim, 0)
    query_block = iota(slim, 1) >> 6
    lower = jnp.zeros(slim, jnp.int32)
    upper = jnp.zeros(slim, jnp.int32)
    for n in range(4):
        lower = jnp.where(query_block == n, bands[0, n], lower)
        upper = jnp.where(query_block == n, bands[1, n], upper)
    banned = (key_block < query_block - lower) | (key_block > query_block + upper)
    bias[...] = jnp.where(banned & (key_block < 4), -1e30, 0.0).astype(BF16)
    wide = (LEN, 128)
    hot[...] = jnp.where((iota(wide, 1) & 63) == (iota(wide, 0) >> 6), 1.0, 0.0).astype(BF16)

    for cp in loads[4:]:
        cp.wait()
    gain_row = gain[...]

    finish(depth)
    for k in range(2):
        rim_depth(0, k)

    for k in range(2):
        finish(top if k else low)
        rim_side(0, k)

        def forward(d, carry, k=k):
            rows = pl.ds(pl.multiple_of(d * 16, 16), 16)
            conv = [
                conv_row(pad, taps, d, h, False) + pad[d + 1, h + 1]
                for h in (2 * k, 2 * k + 1)
            ]
            filt[k, rows] = jnp.concatenate(conv, 0).astype(BF16)
            return carry

        lax.fori_loop(0, DEP, forward, 0)
        for n in range(LEN // 64):
            rows = slice(n * 64, (n + 1) * 64)
            vals = filt[k, rows].astype(F32)
            centred = vals - jnp.sum(vals, -1, keepdims=True) * (1.0 / WID)
            var = jnp.sum(centred * centred, -1, keepdims=True) * (1.0 / WID)
            inv = lax.rsqrt(var + 1e-05)
            xhat = centred * inv
            unit[k, rows] = xhat
            scale[k, rows] = jnp.broadcast_to(inv, (64, 128))
            normed[k, rows] = (xhat * gain_row).astype(BF16)
        send_n[k] = dot_nn(swap[...], normed[k]).astype(BF16)
        exchange(1, k, send_n, col_n)

    exchange(0, 1, send_g, col_g)

    for src, dst in ((wq, wqt), (wk, wkt), (wv, wvt)):
        for n in range(2):
            half = slice(n * LEN, (n + 1) * LEN)
            dst[half] = dot_nt(eye[...], src[:, half]).astype(BF16)

    low_half = iota(wide, 1) < 64
    none = jnp.zeros(slim, BF16)
    ones = jnp.ones((16, LEN), BF16)

    def pair_of(pair, n):
        lanes = pl.ds(pair * 128, 128)
        feats = pl.ds(pair * 128 + n * 64, 64)
        return lanes, feats

    def attend(col):
        arrived(1, col, col_n)
        x = col_n[col]
        k_s[...] = dot_nn(x, wk[...]).astype(BF16)
        query = dot_nt(wqt[...], x).astype(BF16).astype(F32) * 0.125
        qt_s[col] = query.astype(BF16)
        vt_s[...] = dot_nt(wvt[...], x).astype(BF16)

        def heads(pair, carry):
            for n in range(2):
                lanes, feats = pair_of(pair, n)
                k2, qt = k_s[:, lanes], qt_s[col, feats]
                if n == 0:
                    keys = jnp.where(low_half, k2, hot[...])
                    queries = jnp.concatenate([qt, bias[...]], 0)
                else:
                    keys = jnp.where(low_half, hot[...], k2)
                    queries = jnp.concatenate([bias[...], qt], 0)
                scores = dot_nn(keys, queries)
                top = jnp.max(scores, 0, keepdims=True)
                weights = jnp.exp(scores - top).astype(BF16)
                exp_s[col, 2 * pair + n] = weights
                sums = dot_nn(jnp.concatenate([vt_s[feats], ones], 0), weights)
                inv = 1.0 / sums[64:65]
                inv_s[col, 2 * pair + n] = jnp.broadcast_to(inv, (8, LEN))
                at_s[col, feats] = (sums[:64] * inv).astype(BF16)
            return carry

        for pair in range(4):
            heads(pair, 0)
        send_a[col] = dot_nt(eye[...], at_s[col]).astype(BF16)

    def attend_back(col):
        x = col_n[col]
        v_s[...] = dot_nn(x, wv[...]).astype(BF16)
        kt_s[...] = dot_nt(wkt[...], x).astype(BF16)
        arrived(0, col, col_g)
        gt_s[...] = dot_nt(wo[...], col_g[col]).astype(BF16)

        def heads(pair, carry):
            for n in range(2):
                lanes, feats = pair_of(pair, n)
                v2, gt = v_s[:, lanes], gt_s[feats]
                grads = jnp.concatenate([none, gt] if n else [gt, none], 0)
                grad_p = dot_nn(v2, grads)
                gtf = gt.astype(F32)
                centre = jnp.sum(at_s[col, feats].astype(F32) * gtf, 0, keepdims=True)
                weights = exp_s[col, 2 * pair + n]
                inv = inv_s[col, 2 * pair + n][0:1]
                grad_s = (weights.astype(F32) * (grad_p - centre)).astype(BF16)
                gq_s[feats] = (dot_nn(kt_s[feats], grad_s) * (inv * 0.125)).astype(BF16)
                gv_s[feats] = dot_nt((gtf * inv).astype(BF16), weights).astype(BF16)
                query = (qt_s[col, feats].astype(F32) * inv).astype(BF16)
                gk_s[feats] = dot_nt(query, grad_s).astype(BF16)
            return carry

        for pair in range(4):
            heads(pair, 0)
        grads_t = dot_nn(wq[...], gq_s[...]) + dot_nn(wk[...], gk_s[...])
        grads_t = (grads_t + dot_nn(wv[...], gv_s[...])).astype(BF16)
        send_b[col] = dot_nt(eye[...], grads_t).astype(BF16)

    def project(k):
        arrived(3, k, ret_a)
        att = dot_nn(swap[...], ret_a[k]).astype(BF16)
        whole = filt[k].astype(F32) + dot_nn(att, wo[...])
        out[:, k] = whole.astype(BF16).reshape(DEP, 16, WID)
        cp = pltpu.make_async_copy(out.at[:, k], out_h.at[:, k], store_sem.at[0, k])
        cp.start()
        return cp

    attend(0)
    exchange(3, 0, send_a, ret_a)
    attend(1)
    attend_back(0)
    exchange(2, 0, send_b, ret_b)
    attend_back(1)
    exchange(2, 1, send_b, ret_b)
    exchange(3, 1, send_a, ret_a)
    stores = [project(0)]

    depth = []
    sides = []
    for k in range(2):
        arrived(2, k, ret_b)
        unit_grad = dot_nn(swap[...], ret_b[k]) * gain_row
        xhat = unit[k]
        mean = jnp.sum(unit_grad, -1, keepdims=True) * (1.0 / WID)
        along = jnp.sum(unit_grad * xhat, -1, keepdims=True) * (1.0 / WID)
        inv = scale[k][:, 0:1]
        rest = go[:, k].reshape(LEN, WID).astype(F32)
        rounded = (rest + inv * (unit_grad - mean - xhat * along)).astype(BF16)
        grad_f[:, k] = rounded.reshape(DEP, 16, WID)
        values = rounded.astype(F32).reshape(DEP, 2, WIN, WID)
        pad[1 : 1 + DEP, 1 + 2 * k : 3 + 2 * k] = values
        edge[1, k] = values[:, k].reshape(DEP * WIN, WID).astype(BF16)
        new = halo_side(1, k), halo_depth(1, grad_f, k)
        start(new[1] + new[0])
        sides.append(new[0])
        depth.append(new[1])

    stores.append(project(1))

    def adjoint(k, first, count):
        def one(d, carry):
            conv = [
                conv_row(pad, taps, d, h, True) + pad[d + 1, h + 1]
                for h in (2 * k, 2 * k + 1)
            ]
            gt[d, k] = jnp.concatenate(conv, 0).astype(BF16)
            return carry

        lax.fori_loop(first, first + count, one, 0)

    finish(sides[0])
    rim_side(1, 1)
    adjoint(1, 1, DEP - 2)
    for k in range(2):
        finish(depth[k])
        rim_depth(1, k)
    adjoint(1, 0, 1)
    adjoint(1, DEP - 1, 1)
    cp = pltpu.make_async_copy(gt.at[:, 1], grad_h.at[:, 1], store_sem.at[1, 1])
    cp.start()
    stores.append(cp)
    finish(sides[1])
    rim_side(1, 0)
    adjoint(0, 0, DEP)
    cp = pltpu.make_async_copy(gt.at[:, 0], grad_h.at[:, 0], store_sem.at[1, 0])
    cp.start()
    stores.append(cp)
    for kind, src in enumerate((send_g, send_n, send_b, send_a)):
        for col in range(PER):
            sent(kind, col, src)
    finish(stores)


def body(tokens, conv_weight, gain, bands, w_query, w_key, w_value, w_out, grad_out):
    whole = (DEP, 2, 16, WID)
    pair = (PER, LEN, WID)
    hbm = pl.BlockSpec(memory_space=pltpu.HBM)
    scratch = [
        pltpu.SMEM((2, 4), jnp.int32),
        pltpu.VMEM((27, WID), BF16),
        pltpu.VMEM((1, WID), F32),
        pltpu.VMEM(whole, BF16), pltpu.VMEM(whole, BF16),
        *[pltpu.VMEM((WID, WID), BF16) for _ in range(7)],
        pltpu.VMEM((27, WIN, WID), F32),
        pltpu.VMEM((DEP + 2, HGT + 2, WIN, WID), F32),
        pltpu.VMEM((2, 2, DEP * WIN, WID), BF16),
        pltpu.VMEM((2, 2, 2, 16, WID), BF16),
        pltpu.VMEM((2, 2, DEP * WIN, WID), BF16),
        pltpu.VMEM((2, 2, 2, 16, WID), BF16),
        *[pltpu.VMEM(pair, BF16) for _ in range(8)],
        pltpu.VMEM((LEN, LEN), BF16), pltpu.VMEM((LEN, LEN), BF16),
        pltpu.VMEM((64, LEN), BF16), pltpu.VMEM((LEN, 128), BF16),
        pltpu.VMEM(pair, BF16), pltpu.VMEM(pair, BF16),
        pltpu.VMEM(pair, F32),
        pltpu.VMEM((PER, LEN, 128), F32),
        *[pltpu.VMEM(whole, BF16) for _ in range(3)],
        *[pltpu.VMEM((LEN, WID), BF16) for _ in range(2)],
        pltpu.VMEM((PER, WID, LEN), BF16),
        *[pltpu.VMEM((WID, LEN), BF16) for _ in range(3)],
        pltpu.VMEM((PER, WID, LEN), BF16),
        *[pltpu.VMEM((WID, LEN), BF16) for _ in range(3)],
        pltpu.VMEM((PER, 8, LEN, LEN), BF16),
        pltpu.VMEM((PER, 8, 8, LEN), F32),
        pltpu.SemaphoreType.DMA((9,)),
        pltpu.SemaphoreType.DMA((2, 2, 5)), pltpu.SemaphoreType.DMA((2, 2, 5)),
        pltpu.SemaphoreType.DMA((4, PER)), pltpu.SemaphoreType.DMA((4, PER)),
        pltpu.SemaphoreType.DMA((2, 2)),
    ]
    out, grad = pl.pallas_call(
        kernel,
        out_shape=(jax.ShapeDtypeStruct(whole, BF16), jax.ShapeDtypeStruct(whole, BF16)),
        in_specs=[hbm] * 9,
        out_specs=(hbm, hbm),
        scratch_shapes=scratch,
        compiler_params=pltpu.CompilerParams(
            collective_id=0, has_side_effects=True, vmem_limit_bytes=60 * 2**20
        ),
        name="sublayer",
    )(
        bands.T, conv_weight, gain.reshape(1, WID), tokens.reshape(whole),
        grad_out.reshape(whole), w_query, w_key, w_value, w_out,
    )
    return out.reshape(tokens.shape), grad.reshape(tokens.shape)


def solution(mesh):
    slab = P("grp", "inner", None, None)
    in_specs = (slab, P(), P(), P(), P(), P(), P(), P(), slab)
    return jax.shard_map(
        body, mesh=mesh, in_specs=in_specs, out_specs=(slab, slab), check_vma=False
    )
```

```python
import jax
import jax.numpy as jnp
from jax import lax
from jax.experimental import pallas as pl
from jax.experimental.pallas import tpu as pltpu
from jax.sharding import PartitionSpec as P

MESH = pl.DeviceIdType.MESH
F32 = jnp.float32
BF16 = jnp.bfloat16
WID = 512
DEP = 16
HGT = 4
WIN = 8
TOK = DEP * HGT * WIN
COLS = HGT * WIN
LEN = 256
PER = 2


def dot_nn(a, b):
    return lax.dot_general(a, b, (((1,), (0,)), ((), ())), preferred_element_type=F32)


def dot_nt(a, b):
    return lax.dot_general(a, b, (((1,), (1,)), ((), ())), preferred_element_type=F32)


def dot_tn(a, b):
    return lax.dot_general(a, b, (((0,), (0,)), ((), ())), preferred_element_type=F32)


def iota(shape, dim):
    return lax.broadcasted_iota(jnp.int32, shape, dim)


def conv_row(pad, taps, d, h, flip):
    acc = [None, None, None]
    for a in range(3):
        for b in range(3):
            v = pad[d + a, h + b]
            for c in range(3):
                tap = 9 * a + 3 * b + c
                term = taps[26 - tap if flip else tap] * v
                acc[c] = term if acc[c] is None else acc[c] + term
    row = iota((WIN, WID), 0)
    before = jnp.where(row == 0, 0.0, pltpu.roll(acc[0], 1, 0))
    after = jnp.where(row == WIN - 1, 0.0, pltpu.roll(acc[2], WIN - 1, 0))
    return acc[1] + before + after


def kernel(
    bands_h, conv_h, gain_h, tok_h, go_h, wq_h, wk_h, wv_h, wo_h, out_h, grad_h,
    bands, conv_w, gain, tok, go, wq, wk, wv, wo, wqt, wkt, wvt, taps, pad, edge,
    rim_d, rim_h, rim_c, send_n, send_g, col_n, col_g, send_a, send_b, ret_a, ret_b,
    swap, eye, bias, hot, filt, normed, unit, scale, grad_f, out, gt,
    k_s, v_s, qt_s, kt_s, vt_s, gt_s, at_s, gq_s, gk_s, gv_s, exp_s, inv_s, grad_s, mid,
    load_sem, halo_ss, halo_rs, a2a_ss, a2a_rs, store_sem,
):
    g = lax.axis_index("grp")
    i = lax.axis_index("inner")
    ng = lax.axis_size("grp")
    ni = lax.axis_size("inner")
    up_g, dn_g = lax.rem(g + 1, ng), lax.rem(g + ng - 1, ng)
    up_i, dn_i = lax.rem(i + 1, ni), lax.rem(i + ni - 1, ni)

    pairs = (
        (tok_h, tok), (conv_h, conv_w), (go_h, go), (bands_h, bands), (gain_h, gain),
        (wq_h, wq), (wk_h, wk), (wv_h, wv), (wo_h, wo),
    )
    loads = [
        pltpu.make_async_copy(src, dst, load_sem.at[n]) for n, (src, dst) in enumerate(pairs)
    ]
    for cp in loads:
        cp.start()

    barrier = pltpu.get_barrier_semaphore()
    sides = ((g, up_i), (g, dn_i), (up_g, up_i), (up_g, dn_i), (dn_g, up_i), (dn_g, dn_i))

    def greet(step, carry):
        pl.semaphore_signal(
            barrier, inc=1, device_id=(lax.rem(g + step, ng), i), device_id_type=MESH
        )
        return carry

    for peer in sides:
        pl.semaphore_signal(barrier, inc=1, device_id=peer, device_id_type=MESH)
    lax.fori_loop(1, ng, greet, 0)

    last = DEP * WIN - 16

    def halo(phase, k, n, src, dst, dev):
        return pltpu.make_async_remote_copy(
            src_ref=src, dst_ref=dst, send_sem=halo_ss.at[phase, k, n],
            recv_sem=halo_rs.at[phase, k, n], device_id=dev, device_id_type=MESH,
        )

    def halo_depth(phase, body, k):
        return [
            halo(phase, k, 0, body.at[DEP - 1, k], rim_d.at[phase, 0, k], (up_g, i)),
            halo(phase, k, 1, body.at[0, k], rim_d.at[phase, 1, k], (dn_g, i)),
        ]

    def halo_side(phase, k):
        to = up_i if k else dn_i
        side = 1 - k
        return [
            halo(phase, k, 2, edge.at[phase, k], rim_h.at[phase, side], (g, to)),
            halo(
                phase, k, 3, edge.at[phase, k, pl.ds(last, 16)],
                rim_c.at[phase, 0, side], (up_g, to),
            ),
            halo(
                phase, k, 4, edge.at[phase, k, pl.ds(0, 16)],
                rim_c.at[phase, 1, side], (dn_g, to),
            ),
        ]

    def start(copies):
        for cp in copies:
            cp.start()

    def finish(copies):
        for cp in copies:
            cp.wait()

    in_g = (g > 0, g < ng - 1)
    in_i = (i > 0, i < ni - 1)

    def part(ok, val):
        return jnp.where(ok, val.astype(F32), 0.0)

    def rim_depth(phase, k):
        for n in range(2):
            pad[(DEP + 1) * n, 1 + 2 * k : 3 + 2 * k] = part(
                in_g[n], rim_d[phase, n, k]
            ).reshape(2, WIN, WID)

    def rim_side(phase, side):
        h = (HGT + 1) * side
        for n in range(2):
            corner = part(in_g[n] & in_i[side], rim_c[phase, n, side])
            pad[(DEP + 1) * n, h] = corner[:WIN] if n else corner[WIN:]
        pad[1 : 1 + DEP, h] = part(in_i[side], rim_h[phase, side]).reshape(DEP, WIN, WID)

    def own_rows(owner):
        return pl.ds(pl.multiple_of(owner * DEP, DEP), DEP)

    high, chip, core = lax.div(g, 8), lax.rem(lax.div(g, 2), 4), lax.rem(g, 2)
    peers = []
    for step in range(ng - 1):
        far_y, far_x = step < 8, (2, 1, 3, 0)[step // 2 % 4]
        same = 1 - (step + 1) % 2
        p_y = 1 - high if far_y else high
        p_x = lax.rem(chip + far_x, 4) if far_x else chip
        p_c = core if same else 1 - core
        peers.append(p_y * 8 + p_x * 2 + p_c)

    def exchange(kind, col, src, dst):
        for p in peers:
            pltpu.make_async_remote_copy(
                src_ref=src.at[col, own_rows(p)], dst_ref=dst.at[col, own_rows(g)],
                send_sem=a2a_ss.at[kind, col], recv_sem=a2a_rs.at[kind, col],
                device_id=(p, i), device_id_type=MESH,
            ).start()
        pltpu.make_async_copy(
            src.at[col, own_rows(g)], dst.at[col, own_rows(g)], a2a_rs.at[kind, col]
        ).start()

    def arrived(kind, col, dst):
        pltpu.make_async_copy(dst.at[col], dst.at[col], a2a_rs.at[kind, col]).wait()

    def sent(kind, col, src):
        rows = pl.ds(0, LEN - DEP)
        pltpu.make_async_copy(
            src.at[col, rows], src.at[col, rows], a2a_ss.at[kind, col]
        ).wait()

    def filtered(d, h, flip):
        return conv_row(pad, taps, d, h, flip) + pad[d + 1, h + 1]

    def middle(flip, first, count):
        def one(d, carry):
            for k in range(2):
                mid[k, d] = filtered(d, 1 + k, flip)
            return carry

        lax.fori_loop(first, first + count, one, 0, unroll=2 if count > 1 else 1)

    def both_rows(d, k, flip):
        outer = filtered(d, 3 * k, flip)
        rows = [mid[k, d], outer] if k else [outer, mid[k, d]]
        return jnp.concatenate(rows, 0).astype(BF16)

    loads[0].wait()

    def fill(d, carry):
        pad[1 + d, 1 : 1 + HGT] = tok[d].reshape(COLS, WID).astype(F32).reshape(HGT, WIN, WID)
        return carry

    lax.fori_loop(0, DEP, fill, 0)
    for k in range(2):
        edge[0, k] = pad[1 : 1 + DEP, 1 + 3 * k].reshape(DEP * WIN, WID).astype(BF16)
    pl.semaphore_wait(barrier, ng - 1 + len(sides))
    depth = halo_depth(0, tok, 0) + halo_depth(0, tok, 1)
    low, top = halo_side(0, 1), halo_side(0, 0)
    start(depth + low + top)

    square = (LEN, LEN)
    row, lane = iota(square, 0), iota(square, 1)
    swap[...] = jnp.where(lane == (row & 15) * 16 + (row >> 4), 1.0, 0.0).astype(BF16)
    eye[...] = jnp.where(row == lane, 1.0, 0.0).astype(BF16)

    loads[2].wait()
    for k in range(2):
        send_g[k] = dot_nn(swap[...], go[:, k].reshape(LEN, WID)).astype(BF16)

    loads[1].wait()
    conv_f = conv_w[...].astype(F32)
    for n in range(27):
        taps[n] = jnp.broadcast_to(conv_f[n : n + 1], (WIN, WID))

    loads[3].wait()
    slim = (64, LEN)
    key_block = iota(slim, 0)
    query_block = iota(slim, 1) >> 6
    lower = jnp.zeros(slim, jnp.int32)
    upper = jnp.zeros(slim, jnp.int32)
    for n in range(4):
        lower = jnp.where(query_block == n, bands[0, n], lower)
        upper = jnp.where(query_block == n, bands[1, n], upper)
    banned = (key_block < query_block - lower) | (key_block > query_block + upper)
    bias[...] = jnp.where(banned & (key_block < 4), -1e30, 0.0).astype(BF16)
    wide = (LEN, 128)
    hot[...] = jnp.where((iota(wide, 1) & 63) == (iota(wide, 0) >> 6), 1.0, 0.0).astype(BF16)

    for cp in loads[4:]:
        cp.wait()
    gain_row = gain[...]

    middle(False, 1, DEP - 2)
    finish(depth)
    for k in range(2):
        rim_depth(0, k)
    middle(False, 0, 1)
    middle(False, DEP - 1, 1)

    for k in range(2):
        finish(top if k else low)
        rim_side(0, k)

        def forward(d, carry, k=k):
            rows = pl.ds(pl.multiple_of(d * 16, 16), 16)
            filt[k, rows] = both_rows(d, k, False)
            return carry

        lax.fori_loop(0, DEP, forward, 0, unroll=2)
        for n in range(LEN // 64):
            rows = slice(n * 64, (n + 1) * 64)
            vals = filt[k, rows].astype(F32)
            centred = vals - jnp.sum(vals, -1, keepdims=True) * (1.0 / WID)
            var = jnp.sum(centred * centred, -1, keepdims=True) * (1.0 / WID)
            inv = lax.rsqrt(var + 1e-05)
            xhat = centred * inv
            unit[k, rows] = xhat
            scale[k, rows] = jnp.broadcast_to(inv, (64, 128))
            normed[k, rows] = (xhat * gain_row).astype(BF16)
        send_n[k] = dot_nn(swap[...], normed[k]).astype(BF16)
        exchange(1, k, send_n, col_n)

    exchange(0, 0, send_g, col_g)
    exchange(0, 1, send_g, col_g)

    for src, dst in ((wq, wqt), (wk, wkt), (wv, wvt)):
        for n in range(2):
            half = slice(n * LEN, (n + 1) * LEN)
            dst[half] = dot_nt(eye[...], src[:, half]).astype(BF16)

    low_half = iota(wide, 1) < 64
    none = jnp.zeros(slim, BF16)
    ones = jnp.ones((16, LEN), BF16)

    def part_of(head):
        first = head // 2 * 128
        return slice(first, first + 128), slice(head * 64, head * 64 + 64)

    def attend(col):
        arrived(1, col, col_n)
        x = col_n[col]
        k_s[...] = dot_nn(x, wk[...]).astype(BF16)
        query = dot_nt(wqt[...], x).astype(BF16).astype(F32) * 0.125
        qt_s[col] = query.astype(BF16)
        vt_s[...] = dot_nt(wvt[...], x).astype(BF16)

        for head in range(8):
            lanes, feats = part_of(head)
            k2, qt = k_s[:, lanes], qt_s[col, feats]
            if head % 2 == 0:
                keys = jnp.where(low_half, k2, hot[...])
                queries = jnp.concatenate([qt, bias[...]], 0)
            else:
                keys = jnp.where(low_half, hot[...], k2)
                queries = jnp.concatenate([bias[...], qt], 0)
            scores = dot_nn(keys, queries)
            peak = jnp.max(scores, 0, keepdims=True)
            exp_s[col, head] = jnp.exp(scores - peak).astype(BF16)
        for head in range(8):
            lanes, feats = part_of(head)
            sums = dot_nn(jnp.concatenate([vt_s[feats], ones], 0), exp_s[col, head])
            inv = 1.0 / sums[64:65]
            inv_s[col, head] = jnp.broadcast_to(inv, (8, LEN))
            at_s[col, feats] = (sums[:64] * inv).astype(BF16)
        send_a[col] = at_s[col].T

    def attend_back(col):
        x = col_n[col]
        v_s[...] = dot_nn(x, wv[...]).astype(BF16)
        kt_s[...] = dot_nt(wkt[...], x).astype(BF16)
        arrived(0, col, col_g)
        gt_s[...] = dot_nt(wo[...], col_g[col]).astype(BF16)

        for head in range(8):
            lanes, feats = part_of(head)
            v2, gt_h = v_s[:, lanes], gt_s[feats]
            grads = jnp.concatenate([none, gt_h] if head % 2 else [gt_h, none], 0)
            grad_p = dot_nn(v2, grads)
            dots = at_s[col, feats].astype(F32) * gt_h.astype(F32)
            centre = jnp.sum(dots, 0, keepdims=True)
            weights = exp_s[col, head].astype(F32)
            grad_s[head] = (weights * (grad_p - centre)).astype(BF16)
        for head in range(8):
            lanes, feats = part_of(head)
            inv = inv_s[col, head][0:1]
            gt_h = (gt_s[feats].astype(F32) * inv).astype(BF16)
            gv_s[feats] = dot_nt(gt_h, exp_s[col, head]).astype(BF16)
            query = (qt_s[col, feats].astype(F32) * inv).astype(BF16)
            gk_s[feats] = dot_nt(query, grad_s[head]).astype(BF16)
            key = dot_nn(kt_s[feats], grad_s[head])
            gq_s[feats] = (key * (inv * 0.125)).astype(BF16)
        send_b[col] = (
            dot_tn(gq_s[...], wqt[...]) + dot_tn(gk_s[...], wkt[...]) + dot_tn(gv_s[...], wvt[...])
        ).astype(BF16)

    def project(k):
        arrived(3, k, ret_a)
        att = dot_nn(swap[...], ret_a[k]).astype(BF16)
        whole = filt[k].astype(F32) + dot_nn(att, wo[...])
        out[:, k] = whole.astype(BF16).reshape(DEP, 16, WID)
        cp = pltpu.make_async_copy(out.at[:, k], out_h.at[:, k], store_sem.at[0, k])
        cp.start()
        return cp

    attend(0)
    exchange(3, 0, send_a, ret_a)
    attend(1)
    exchange(3, 1, send_a, ret_a)
    attend_back(0)
    exchange(2, 0, send_b, ret_b)
    attend_back(1)
    exchange(2, 1, send_b, ret_b)
    stores = [project(0)]

    depth = []
    sides = []
    for k in range(2):
        arrived(2, k, ret_b)
        unit_grad = dot_nn(swap[...], ret_b[k]) * gain_row
        xhat = unit[k]
        mean = jnp.sum(unit_grad, -1, keepdims=True) * (1.0 / WID)
        along = jnp.sum(unit_grad * xhat, -1, keepdims=True) * (1.0 / WID)
        inv = scale[k][:, 0:1]
        rest = go[:, k].reshape(LEN, WID).astype(F32)
        rounded = (rest + inv * (unit_grad - mean - xhat * along)).astype(BF16)
        grad_f[:, k] = rounded.reshape(DEP, 16, WID)
        values = rounded.astype(F32).reshape(DEP, 2, WIN, WID)
        pad[1 : 1 + DEP, 1 + 2 * k : 3 + 2 * k] = values
        edge[1, k] = values[:, k].reshape(DEP * WIN, WID).astype(BF16)
        new = halo_side(1, k), halo_depth(1, grad_f, k)
        start(new[1] + new[0])
        sides.append(new[0])
        depth.append(new[1])

    stores.append(project(1))

    def adjoint(k, first, count):
        def one(d, carry):
            gt[d, k] = both_rows(d, k, True)
            return carry

        lax.fori_loop(first, first + count, one, 0, unroll=2 if count > 1 else 1)

    middle(True, 1, DEP - 2)
    finish(sides[0])
    rim_side(1, 1)
    adjoint(1, 1, DEP - 2)
    for k in range(2):
        finish(depth[k])
        rim_depth(1, k)
    for d in (0, DEP - 1):
        middle(True, d, 1)
        adjoint(1, d, 1)
    cp = pltpu.make_async_copy(gt.at[:, 1], grad_h.at[:, 1], store_sem.at[1, 1])
    cp.start()
    stores.append(cp)
    finish(sides[1])
    rim_side(1, 0)
    adjoint(0, 0, DEP)
    cp = pltpu.make_async_copy(gt.at[:, 0], grad_h.at[:, 0], store_sem.at[1, 0])
    cp.start()
    stores.append(cp)
    for kind, src in enumerate((send_g, send_n, send_b, send_a)):
        for col in range(PER):
            sent(kind, col, src)
    finish(stores)


def hand_over(out_in, grad_in, out_ref, grad_ref, held, in_sem, out_sem):
    moves = []
    for n, (src, dst) in enumerate(((out_in, out_ref), (grad_in, grad_ref))):
        for half in range(2):
            rows = pl.ds(half * DEP // 2, DEP // 2)
            moves.append((
                pltpu.make_async_copy(src.at[rows], held.at[n, rows], in_sem.at[n, half]),
                pltpu.make_async_copy(held.at[n, rows], dst.at[rows], out_sem.at[n, half]),
            ))
    for load, _ in moves:
        load.start()
    for load, store in moves:
        load.wait()
        store.start()
    for _, store in moves:
        store.wait()


def body(tokens, conv_weight, gain, bands, w_query, w_key, w_value, w_out, grad_out):
    whole = (DEP, 2, 16, WID)
    pair = (PER, LEN, WID)
    hbm = pl.BlockSpec(memory_space=pltpu.HBM)
    scratch = [
        pltpu.SMEM((2, 4), jnp.int32),
        pltpu.VMEM((27, WID), BF16),
        pltpu.VMEM((1, WID), F32),
        pltpu.VMEM(whole, BF16), pltpu.VMEM(whole, BF16),
        *[pltpu.VMEM((WID, WID), BF16) for _ in range(7)],
        pltpu.VMEM((27, WIN, WID), F32),
        pltpu.VMEM((DEP + 2, HGT + 2, WIN, WID), F32),
        pltpu.VMEM((2, 2, DEP * WIN, WID), BF16),
        pltpu.VMEM((2, 2, 2, 16, WID), BF16),
        pltpu.VMEM((2, 2, DEP * WIN, WID), BF16),
        pltpu.VMEM((2, 2, 2, 16, WID), BF16),
        *[pltpu.VMEM(pair, BF16) for _ in range(8)],
        pltpu.VMEM((LEN, LEN), BF16), pltpu.VMEM((LEN, LEN), BF16),
        pltpu.VMEM((64, LEN), BF16), pltpu.VMEM((LEN, 128), BF16),
        pltpu.VMEM(pair, BF16), pltpu.VMEM(pair, BF16),
        pltpu.VMEM(pair, F32),
        pltpu.VMEM((PER, LEN, 128), F32),
        *[pltpu.VMEM(whole, BF16) for _ in range(3)],
        *[pltpu.VMEM((LEN, WID), BF16) for _ in range(2)],
        pltpu.VMEM((PER, WID, LEN), BF16),
        *[pltpu.VMEM((WID, LEN), BF16) for _ in range(3)],
        pltpu.VMEM((PER, WID, LEN), BF16),
        *[pltpu.VMEM((WID, LEN), BF16) for _ in range(3)],
        pltpu.VMEM((PER, 8, LEN, LEN), BF16),
        pltpu.VMEM((PER, 8, 8, LEN), F32),
        pltpu.VMEM((8, LEN, LEN), BF16),
        pltpu.VMEM((2, DEP, WIN, WID), F32),
        pltpu.SemaphoreType.DMA((9,)),
        pltpu.SemaphoreType.DMA((2, 2, 5)), pltpu.SemaphoreType.DMA((2, 2, 5)),
        pltpu.SemaphoreType.DMA((4, PER)), pltpu.SemaphoreType.DMA((4, PER)),
        pltpu.SemaphoreType.DMA((2, 2)),
    ]
    made = pl.pallas_call(
        kernel,
        out_shape=(jax.ShapeDtypeStruct(whole, BF16), jax.ShapeDtypeStruct(whole, BF16)),
        in_specs=[hbm] * 9,
        out_specs=(hbm, hbm),
        scratch_shapes=scratch,
        compiler_params=pltpu.CompilerParams(
            collective_id=0, has_side_effects=True, vmem_limit_bytes=60 * 2**20
        ),
        name="sublayer",
    )(
        bands.T, conv_weight, gain.reshape(1, WID), tokens.reshape(whole),
        grad_out.reshape(whole), w_query, w_key, w_value, w_out,
    )
    out, grad = pl.pallas_call(
        hand_over,
        out_shape=(jax.ShapeDtypeStruct(whole, BF16), jax.ShapeDtypeStruct(whole, BF16)),
        in_specs=[hbm] * 2,
        out_specs=(hbm, hbm),
        scratch_shapes=[
            pltpu.VMEM((2, *whole), BF16),
            pltpu.SemaphoreType.DMA((2, 2)), pltpu.SemaphoreType.DMA((2, 2)),
        ],
        compiler_params=pltpu.CompilerParams(vmem_limit_bytes=60 * 2**20),
        name="hand_over",
    )(*made)
    return out.reshape(tokens.shape), grad.reshape(tokens.shape)


def solution(mesh):
    slab = P("grp", "inner", None, None)
    in_specs = (slab, P(), P(), P(), P(), P(), P(), P(), slab)
    return jax.shard_map(
        body, mesh=mesh, in_specs=in_specs, out_specs=(slab, slab), check_vma=False
    )
```

```python
import jax
import jax.numpy as jnp
from jax import lax
from jax.experimental import pallas as pl
from jax.experimental.pallas import tpu as pltpu
from jax.sharding import PartitionSpec as P

MESH = pl.DeviceIdType.MESH
F32 = jnp.float32
BF16 = jnp.bfloat16
WID = 512
DEP = 16
HGT = 4
WIN = 8
TOK = DEP * HGT * WIN
COLS = HGT * WIN
LEN = 256
PER = 2


def dot_nn(a, b):
    return lax.dot_general(a, b, (((1,), (0,)), ((), ())), preferred_element_type=F32)


def dot_nt(a, b):
    return lax.dot_general(a, b, (((1,), (1,)), ((), ())), preferred_element_type=F32)


def dot_tn(a, b):
    return lax.dot_general(a, b, (((0,), (0,)), ((), ())), preferred_element_type=F32)


def iota(shape, dim):
    return lax.broadcasted_iota(jnp.int32, shape, dim)


def conv_row(pad, taps, d, h, flip):
    acc = [None, None, None]
    for a in range(3):
        for b in range(3):
            v = pad[d + a, h + b]
            for c in range(3):
                tap = 9 * a + 3 * b + c
                term = taps[26 - tap if flip else tap] * v
                acc[c] = term if acc[c] is None else acc[c] + term
    row = iota((WIN, WID), 0)
    before = jnp.where(row == 0, 0.0, pltpu.roll(acc[0], 1, 0))
    after = jnp.where(row == WIN - 1, 0.0, pltpu.roll(acc[2], WIN - 1, 0))
    return acc[1] + before + after


def kernel(
    bands_h, conv_h, gain_h, tok_h, go_h, wq_h, wk_h, wv_h, wo_h, out_h, grad_h,
    bands, conv_w, gain, tok, go, wq, wk, wv, wo, wqt, wkt, wvt, taps, pad, edge,
    rim_d, rim_h, rim_c, send_n, send_g, col_n, col_g, send_a, send_b, ret_a, ret_b,
    swap, eye, bias, hot, filt, normed, unit, scale, grad_f, out, gt,
    k_s, v_s, qt_s, kt_s, vt_s, gt_s, at_s, gq_s, gk_s, gv_s, exp_s, inv_s, grad_s, mid,
    load_sem, halo_ss, halo_rs, a2a_ss, a2a_rs, store_sem,
):
    g = lax.axis_index("grp")
    i = lax.axis_index("inner")
    ng = lax.axis_size("grp")
    ni = lax.axis_size("inner")
    up_g, dn_g = lax.rem(g + 1, ng), lax.rem(g + ng - 1, ng)
    up_i, dn_i = lax.rem(i + 1, ni), lax.rem(i + ni - 1, ni)

    pairs = (
        (tok_h.at[:, 1], tok.at[:, 1]), (tok_h.at[:, 0], tok.at[:, 0]),
        (conv_h, conv_w), (go_h, go), (bands_h, bands), (gain_h, gain),
        (wq_h, wq), (wk_h, wk), (wv_h, wv), (wo_h, wo),
    )
    loads = [
        pltpu.make_async_copy(src, dst, load_sem.at[n]) for n, (src, dst) in enumerate(pairs)
    ]
    for cp in loads:
        cp.start()

    barrier = pltpu.get_barrier_semaphore()
    sides = ((g, up_i), (g, dn_i), (up_g, up_i), (up_g, dn_i), (dn_g, up_i), (dn_g, dn_i))

    def greet(step, carry):
        pl.semaphore_signal(
            barrier, inc=1, device_id=(lax.rem(g + step, ng), i), device_id_type=MESH
        )
        return carry

    for peer in sides:
        pl.semaphore_signal(barrier, inc=1, device_id=peer, device_id_type=MESH)
    lax.fori_loop(1, ng, greet, 0)

    last = DEP * WIN - 16

    def halo(phase, k, n, src, dst, dev):
        return pltpu.make_async_remote_copy(
            src_ref=src, dst_ref=dst, send_sem=halo_ss.at[phase, k, n],
            recv_sem=halo_rs.at[phase, k, n], device_id=dev, device_id_type=MESH,
        )

    def halo_depth(phase, body, k):
        return [
            halo(phase, k, 0, body.at[DEP - 1, k], rim_d.at[phase, 0, k], (up_g, i)),
            halo(phase, k, 1, body.at[0, k], rim_d.at[phase, 1, k], (dn_g, i)),
        ]

    def halo_side(phase, k):
        to = up_i if k else dn_i
        side = 1 - k
        return [
            halo(phase, k, 2, edge.at[phase, k], rim_h.at[phase, side], (g, to)),
            halo(
                phase, k, 3, edge.at[phase, k, pl.ds(last, 16)],
                rim_c.at[phase, 0, side], (up_g, to),
            ),
            halo(
                phase, k, 4, edge.at[phase, k, pl.ds(0, 16)],
                rim_c.at[phase, 1, side], (dn_g, to),
            ),
        ]

    def start(copies):
        for cp in copies:
            cp.start()

    def finish(copies):
        for cp in copies:
            cp.wait()

    in_g = (g > 0, g < ng - 1)
    in_i = (i > 0, i < ni - 1)

    def part(ok, val):
        return jnp.where(ok, val.astype(F32), 0.0)

    def rim_depth(phase, k):
        for n in range(2):
            pad[(DEP + 1) * n, 1 + 2 * k : 3 + 2 * k] = part(
                in_g[n], rim_d[phase, n, k]
            ).reshape(2, WIN, WID)

    def rim_side(phase, side):
        h = (HGT + 1) * side
        for n in range(2):
            corner = part(in_g[n] & in_i[side], rim_c[phase, n, side])
            pad[(DEP + 1) * n, h] = corner[:WIN] if n else corner[WIN:]
        pad[1 : 1 + DEP, h] = part(in_i[side], rim_h[phase, side]).reshape(DEP, WIN, WID)

    def own_rows(owner):
        return pl.ds(pl.multiple_of(owner * DEP, DEP), DEP)

    high, chip, core = lax.div(g, 8), lax.rem(lax.div(g, 2), 4), lax.rem(g, 2)
    peers = []
    for step in range(ng - 1):
        far_y, far_x = step < 8, (2, 1, 3, 0)[step // 2 % 4]
        same = 1 - (step + 1) % 2
        p_y = 1 - high if far_y else high
        p_x = lax.rem(chip + far_x, 4) if far_x else chip
        p_c = core if same else 1 - core
        peers.append(p_y * 8 + p_x * 2 + p_c)

    def exchange(kind, col, src, dst):
        for p in peers:
            pltpu.make_async_remote_copy(
                src_ref=src.at[col, own_rows(p)], dst_ref=dst.at[col, own_rows(g)],
                send_sem=a2a_ss.at[kind, col], recv_sem=a2a_rs.at[kind, col],
                device_id=(p, i), device_id_type=MESH,
            ).start()
        pltpu.make_async_copy(
            src.at[col, own_rows(g)], dst.at[col, own_rows(g)], a2a_rs.at[kind, col]
        ).start()

    def arrived(kind, col, dst):
        pltpu.make_async_copy(dst.at[col], dst.at[col], a2a_rs.at[kind, col]).wait()

    def sent(kind, col, src):
        rows = pl.ds(0, LEN - DEP)
        pltpu.make_async_copy(
            src.at[col, rows], src.at[col, rows], a2a_ss.at[kind, col]
        ).wait()

    def filtered(d, h, flip):
        return conv_row(pad, taps, d, h, flip) + pad[d + 1, h + 1]

    def middle(flip, first, count):
        def one(d, carry):
            for k in range(2):
                mid[k, d] = filtered(d, 1 + k, flip)
            return carry

        lax.fori_loop(first, first + count, one, 0, unroll=2 if count > 1 else 1)

    def both_rows(d, k, flip):
        outer = filtered(d, 3 * k, flip)
        rows = [mid[k, d], outer] if k else [outer, mid[k, d]]
        return jnp.concatenate(rows, 0).astype(BF16)

    def fill(d, carry):
        pad[1 + d, 1 : 1 + HGT] = tok[d].reshape(COLS, WID).astype(F32).reshape(HGT, WIN, WID)
        return carry

    def stage(k):
        rows = tok[:, k].astype(F32).reshape(DEP, 2, WIN, WID)
        edge[0, k] = rows[:, k].reshape(DEP * WIN, WID).astype(BF16)

    loads[0].wait()
    stage(1)
    loads[1].wait()
    stage(0)
    pl.semaphore_wait(barrier, ng - 1 + len(sides))
    depth = halo_depth(0, tok, 0) + halo_depth(0, tok, 1)
    low, top = halo_side(0, 1), halo_side(0, 0)
    start(depth + low + top)
    lax.fori_loop(0, DEP, fill, 0)

    square = (LEN, LEN)
    row, lane = iota(square, 0), iota(square, 1)
    swap[...] = jnp.where(lane == (row & 15) * 16 + (row >> 4), 1.0, 0.0).astype(BF16)
    eye[...] = jnp.where(row == lane, 1.0, 0.0).astype(BF16)

    loads[3].wait()
    for k in range(2):
        send_g[k] = dot_nn(swap[...], go[:, k].reshape(LEN, WID)).astype(BF16)

    loads[2].wait()
    conv_f = conv_w[...].astype(F32)
    for n in range(27):
        taps[n] = jnp.broadcast_to(conv_f[n : n + 1], (WIN, WID))

    loads[4].wait()
    slim = (64, LEN)
    key_block = iota(slim, 0)
    query_block = iota(slim, 1) >> 6
    lower = jnp.zeros(slim, jnp.int32)
    upper = jnp.zeros(slim, jnp.int32)
    for n in range(4):
        lower = jnp.where(query_block == n, bands[0, n], lower)
        upper = jnp.where(query_block == n, bands[1, n], upper)
    banned = (key_block < query_block - lower) | (key_block > query_block + upper)
    bias[...] = jnp.where(banned & (key_block < 4), -1e30, 0.0).astype(BF16)
    wide = (LEN, 128)
    hot[...] = jnp.where((iota(wide, 1) & 63) == (iota(wide, 0) >> 6), 1.0, 0.0).astype(BF16)

    for cp in loads[5:]:
        cp.wait()
    gain_row = gain[...]

    middle(False, 1, DEP - 2)
    finish(depth)
    for k in range(2):
        rim_depth(0, k)
    middle(False, 0, 1)
    middle(False, DEP - 1, 1)

    for k in range(2):
        finish(top if k else low)
        if k == 0:
            exchange(0, 0, send_g, col_g)
        rim_side(0, k)

        def forward(d, carry, k=k):
            rows = pl.ds(pl.multiple_of(d * 16, 16), 16)
            filt[k, rows] = both_rows(d, k, False)
            return carry

        lax.fori_loop(0, DEP, forward, 0, unroll=2)
        for n in range(LEN // 64):
            rows = slice(n * 64, (n + 1) * 64)
            vals = filt[k, rows].astype(F32)
            centred = vals - jnp.sum(vals, -1, keepdims=True) * (1.0 / WID)
            var = jnp.sum(centred * centred, -1, keepdims=True) * (1.0 / WID)
            inv = lax.rsqrt(var + 1e-05)
            xhat = centred * inv
            unit[k, rows] = xhat
            scale[k, rows] = jnp.broadcast_to(inv, (64, 128))
            normed[k, rows] = (xhat * gain_row).astype(BF16)
        send_n[k] = dot_nn(swap[...], normed[k]).astype(BF16)
        exchange(1, k, send_n, col_n)

    exchange(0, 1, send_g, col_g)

    for src, dst in ((wq, wqt), (wk, wkt), (wv, wvt)):
        for n in range(2):
            half = slice(n * LEN, (n + 1) * LEN)
            dst[half] = dot_nt(eye[...], src[:, half]).astype(BF16)

    low_half = iota(wide, 1) < 64
    none = jnp.zeros(slim, BF16)
    ones = jnp.ones((16, LEN), BF16)

    def part_of(head):
        first = head // 2 * 128
        return slice(first, first + 128), slice(head * 64, head * 64 + 64)

    def attend(col):
        arrived(1, col, col_n)
        x = col_n[col]
        k_s[...] = dot_nn(x, wk[...]).astype(BF16)
        query = dot_nt(wqt[...], x).astype(BF16).astype(F32) * 0.125
        qt_s[col] = query.astype(BF16)
        vt_s[...] = dot_nt(wvt[...], x).astype(BF16)

        for head in range(8):
            lanes, feats = part_of(head)
            k2, qt = k_s[:, lanes], qt_s[col, feats]
            if head % 2 == 0:
                keys = jnp.where(low_half, k2, hot[...])
                queries = jnp.concatenate([qt, bias[...]], 0)
            else:
                keys = jnp.where(low_half, hot[...], k2)
                queries = jnp.concatenate([bias[...], qt], 0)
            scores = dot_nn(keys, queries)
            peak = jnp.max(scores, 0, keepdims=True)
            exp_s[col, head] = jnp.exp(scores - peak).astype(BF16)
        for head in range(8):
            lanes, feats = part_of(head)
            sums = dot_nn(jnp.concatenate([vt_s[feats], ones], 0), exp_s[col, head])
            inv = 1.0 / sums[64:65]
            inv_s[col, head] = jnp.broadcast_to(inv, (8, LEN))
            at_s[col, feats] = (sums[:64] * inv).astype(BF16)
        send_a[col] = at_s[col].T

    def attend_back(col):
        x = col_n[col]
        v_s[...] = dot_nn(x, wv[...]).astype(BF16)
        kt_s[...] = dot_nt(wkt[...], x).astype(BF16)
        arrived(0, col, col_g)
        gt_s[...] = dot_nt(wo[...], col_g[col]).astype(BF16)

        for head in range(8):
            lanes, feats = part_of(head)
            v2, gt_h = v_s[:, lanes], gt_s[feats]
            grads = jnp.concatenate([none, gt_h] if head % 2 else [gt_h, none], 0)
            grad_p = dot_nn(v2, grads)
            dots = at_s[col, feats].astype(F32) * gt_h.astype(F32)
            centre = jnp.sum(dots, 0, keepdims=True)
            weights = exp_s[col, head].astype(F32)
            grad_s[head] = (weights * (grad_p - centre)).astype(BF16)
        for head in range(8):
            lanes, feats = part_of(head)
            inv = inv_s[col, head][0:1]
            gt_h = (gt_s[feats].astype(F32) * inv).astype(BF16)
            gv_s[feats] = dot_nt(gt_h, exp_s[col, head]).astype(BF16)
            query = (qt_s[col, feats].astype(F32) * inv).astype(BF16)
            gk_s[feats] = dot_nt(query, grad_s[head]).astype(BF16)
            key = dot_nn(kt_s[feats], grad_s[head])
            gq_s[feats] = (key * (inv * 0.125)).astype(BF16)
        send_b[col] = (
            dot_tn(gq_s[...], wqt[...]) + dot_tn(gk_s[...], wkt[...]) + dot_tn(gv_s[...], wvt[...])
        ).astype(BF16)

    def project(k):
        arrived(3, k, ret_a)
        att = dot_nn(swap[...], ret_a[k]).astype(BF16)
        whole = filt[k].astype(F32) + dot_nn(att, wo[...])
        out[:, k] = whole.astype(BF16).reshape(DEP, 16, WID)
        cp = pltpu.make_async_copy(out.at[:, k], out_h.at[:, k], store_sem.at[0, k])
        cp.start()
        return cp

    attend(0)
    exchange(3, 0, send_a, ret_a)
    attend(1)
    exchange(3, 1, send_a, ret_a)
    attend_back(0)
    exchange(2, 0, send_b, ret_b)
    attend_back(1)
    exchange(2, 1, send_b, ret_b)
    stores = [project(0)]

    depth = []
    sides = []
    for k in range(2):
        arrived(2, k, ret_b)
        unit_grad = dot_nn(swap[...], ret_b[k]) * gain_row
        xhat = unit[k]
        mean = jnp.sum(unit_grad, -1, keepdims=True) * (1.0 / WID)
        along = jnp.sum(unit_grad * xhat, -1, keepdims=True) * (1.0 / WID)
        inv = scale[k][:, 0:1]
        rest = go[:, k].reshape(LEN, WID).astype(F32)
        rounded = (rest + inv * (unit_grad - mean - xhat * along)).astype(BF16)
        grad_f[:, k] = rounded.reshape(DEP, 16, WID)
        values = rounded.astype(F32).reshape(DEP, 2, WIN, WID)
        pad[1 : 1 + DEP, 1 + 2 * k : 3 + 2 * k] = values
        edge[1, k] = values[:, k].reshape(DEP * WIN, WID).astype(BF16)
        new = halo_side(1, k), halo_depth(1, grad_f, k)
        start(new[1] + new[0])
        sides.append(new[0])
        depth.append(new[1])

    stores.append(project(1))

    def adjoint(k, first, count):
        def one(d, carry):
            gt[d, k] = both_rows(d, k, True)
            return carry

        lax.fori_loop(first, first + count, one, 0, unroll=2 if count > 1 else 1)

    middle(True, 1, DEP - 2)
    finish(sides[0])
    rim_side(1, 1)
    adjoint(1, 1, DEP - 2)
    for k in range(2):
        finish(depth[k])
        rim_depth(1, k)
    for d in (0, DEP - 1):
        middle(True, d, 1)
        adjoint(1, d, 1)
    cp = pltpu.make_async_copy(gt.at[:, 1], grad_h.at[:, 1], store_sem.at[1, 1])
    cp.start()
    stores.append(cp)
    finish(sides[1])
    rim_side(1, 0)
    adjoint(0, 0, DEP)
    cp = pltpu.make_async_copy(gt.at[:, 0], grad_h.at[:, 0], store_sem.at[1, 0])
    cp.start()
    stores.append(cp)
    for kind, src in enumerate((send_g, send_n, send_b, send_a)):
        for col in range(PER):
            sent(kind, col, src)
    finish(stores)


def hand_over(out_in, grad_in, out_ref, grad_ref, held, in_sem, out_sem):
    moves = []
    for n, (src, dst) in enumerate(((out_in, out_ref), (grad_in, grad_ref))):
        for half in range(2):
            rows = pl.ds(half * DEP // 2, DEP // 2)
            moves.append((
                pltpu.make_async_copy(src.at[rows], held.at[n, rows], in_sem.at[n, half]),
                pltpu.make_async_copy(held.at[n, rows], dst.at[rows], out_sem.at[n, half]),
            ))
    for load, _ in moves:
        load.start()
    for load, store in moves:
        load.wait()
        store.start()
    for _, store in moves:
        store.wait()


def body(tokens, conv_weight, gain, bands, w_query, w_key, w_value, w_out, grad_out):
    whole = (DEP, 2, 16, WID)
    pair = (PER, LEN, WID)
    hbm = pl.BlockSpec(memory_space=pltpu.HBM)
    scratch = [
        pltpu.SMEM((2, 4), jnp.int32),
        pltpu.VMEM((27, WID), BF16),
        pltpu.VMEM((1, WID), F32),
        pltpu.VMEM(whole, BF16), pltpu.VMEM(whole, BF16),
        *[pltpu.VMEM((WID, WID), BF16) for _ in range(7)],
        pltpu.VMEM((27, WIN, WID), F32),
        pltpu.VMEM((DEP + 2, HGT + 2, WIN, WID), F32),
        pltpu.VMEM((2, 2, DEP * WIN, WID), BF16),
        pltpu.VMEM((2, 2, 2, 16, WID), BF16),
        pltpu.VMEM((2, 2, DEP * WIN, WID), BF16),
        pltpu.VMEM((2, 2, 2, 16, WID), BF16),
        *[pltpu.VMEM(pair, BF16) for _ in range(8)],
        pltpu.VMEM((LEN, LEN), BF16), pltpu.VMEM((LEN, LEN), BF16),
        pltpu.VMEM((64, LEN), BF16), pltpu.VMEM((LEN, 128), BF16),
        pltpu.VMEM(pair, BF16), pltpu.VMEM(pair, BF16),
        pltpu.VMEM(pair, F32),
        pltpu.VMEM((PER, LEN, 128), F32),
        *[pltpu.VMEM(whole, BF16) for _ in range(3)],
        *[pltpu.VMEM((LEN, WID), BF16) for _ in range(2)],
        pltpu.VMEM((PER, WID, LEN), BF16),
        *[pltpu.VMEM((WID, LEN), BF16) for _ in range(3)],
        pltpu.VMEM((PER, WID, LEN), BF16),
        *[pltpu.VMEM((WID, LEN), BF16) for _ in range(3)],
        pltpu.VMEM((PER, 8, LEN, LEN), BF16),
        pltpu.VMEM((PER, 8, 8, LEN), F32),
        pltpu.VMEM((8, LEN, LEN), BF16),
        pltpu.VMEM((2, DEP, WIN, WID), F32),
        pltpu.SemaphoreType.DMA((10,)),
        pltpu.SemaphoreType.DMA((2, 2, 5)), pltpu.SemaphoreType.DMA((2, 2, 5)),
        pltpu.SemaphoreType.DMA((4, PER)), pltpu.SemaphoreType.DMA((4, PER)),
        pltpu.SemaphoreType.DMA((2, 2)),
    ]
    made = pl.pallas_call(
        kernel,
        out_shape=(jax.ShapeDtypeStruct(whole, BF16), jax.ShapeDtypeStruct(whole, BF16)),
        in_specs=[hbm] * 9,
        out_specs=(hbm, hbm),
        scratch_shapes=scratch,
        compiler_params=pltpu.CompilerParams(
            collective_id=0, has_side_effects=True, vmem_limit_bytes=60 * 2**20
        ),
        name="sublayer",
    )(
        bands.T, conv_weight, gain.reshape(1, WID), tokens.reshape(whole),
        grad_out.reshape(whole), w_query, w_key, w_value, w_out,
    )
    out, grad = pl.pallas_call(
        hand_over,
        out_shape=(jax.ShapeDtypeStruct(whole, BF16), jax.ShapeDtypeStruct(whole, BF16)),
        in_specs=[hbm] * 2,
        out_specs=(hbm, hbm),
        scratch_shapes=[
            pltpu.VMEM((2, *whole), BF16),
            pltpu.SemaphoreType.DMA((2, 2)), pltpu.SemaphoreType.DMA((2, 2)),
        ],
        compiler_params=pltpu.CompilerParams(vmem_limit_bytes=60 * 2**20),
        name="hand_over",
    )(*made)
    return out.reshape(tokens.shape), grad.reshape(tokens.shape)


def solution(mesh):
    slab = P("grp", "inner", None, None)
    in_specs = (slab, P(), P(), P(), P(), P(), P(), P(), slab)
    return jax.shard_map(
        body, mesh=mesh, in_specs=in_specs, out_specs=(slab, slab), check_vma=False
    )
```

```python
import jax
import jax.numpy as jnp
from jax import lax
from jax.experimental import pallas as pl
from jax.experimental.pallas import tpu as pltpu
from jax.sharding import PartitionSpec as P

MESH = pl.DeviceIdType.MESH
F32 = jnp.float32
BF16 = jnp.bfloat16
WID = 512
DEP = 16
HGT = 4
WIN = 8
TOK = DEP * HGT * WIN
COLS = HGT * WIN
LEN = 256
PER = 2


def dot_nn(a, b):
    return lax.dot_general(a, b, (((1,), (0,)), ((), ())), preferred_element_type=F32)


def dot_nt(a, b):
    return lax.dot_general(a, b, (((1,), (1,)), ((), ())), preferred_element_type=F32)


def dot_tn(a, b):
    return lax.dot_general(a, b, (((0,), (0,)), ((), ())), preferred_element_type=F32)


def iota(shape, dim):
    return lax.broadcasted_iota(jnp.int32, shape, dim)


def conv_row(pad, taps, d, h, flip):
    acc = [None, None, None]
    for a in range(3):
        for b in range(3):
            v = pad[d + a, h + b]
            for c in range(3):
                tap = 9 * a + 3 * b + c
                term = taps[26 - tap if flip else tap] * v
                acc[c] = term if acc[c] is None else acc[c] + term
    row = iota((WIN, WID), 0)
    before = jnp.where(row == 0, 0.0, pltpu.roll(acc[0], 1, 0))
    after = jnp.where(row == WIN - 1, 0.0, pltpu.roll(acc[2], WIN - 1, 0))
    return acc[1] + before + after


def kernel(
    bands_h, conv_h, gain_h, tok_h, go_h, wq_h, wk_h, wv_h, wo_h, out_h, grad_h,
    bands, conv_w, gain, tok, go, wq, wk, wv, wo, wqt, wkt, wvt, taps, pad, edge,
    rim_d, rim_h, rim_c, send_n, send_g, col_n, col_g, send_a, send_b, ret_a, ret_b,
    swap, eye, bias, hot, filt, normed, unit, scale, grad_f, out, gt,
    k_s, v_s, qt_s, kt_s, vt_s, gt_s, at_s, gq_s, gk_s, gv_s, exp_s, inv_s, grad_s, mid,
    load_sem, halo_ss, halo_rs, a2a_ss, a2a_rs, store_sem,
):
    g = lax.axis_index("grp")
    i = lax.axis_index("inner")
    ng = lax.axis_size("grp")
    ni = lax.axis_size("inner")
    up_g, dn_g = lax.rem(g + 1, ng), lax.rem(g + ng - 1, ng)
    up_i, dn_i = lax.rem(i + 1, ni), lax.rem(i + ni - 1, ni)

    pairs = (
        (tok_h.at[:, 1], tok.at[:, 1]), (tok_h.at[:, 0], tok.at[:, 0]),
        (conv_h, conv_w), (go_h, go), (bands_h, bands), (gain_h, gain),
        (wq_h, wq), (wk_h, wk), (wv_h, wv), (wo_h, wo),
    )
    loads = [
        pltpu.make_async_copy(src, dst, load_sem.at[n]) for n, (src, dst) in enumerate(pairs)
    ]
    for cp in loads:
        cp.start()

    barrier = pltpu.get_barrier_semaphore()
    sides = ((g, up_i), (g, dn_i), (up_g, up_i), (up_g, dn_i), (dn_g, up_i), (dn_g, dn_i))

    def greet(step, carry):
        pl.semaphore_signal(
            barrier, inc=1, device_id=(lax.rem(g + step, ng), i), device_id_type=MESH
        )
        return carry

    for peer in sides:
        pl.semaphore_signal(barrier, inc=1, device_id=peer, device_id_type=MESH)
    lax.fori_loop(1, ng, greet, 0)

    last = DEP * WIN - 16

    def halo(phase, k, n, src, dst, dev):
        return pltpu.make_async_remote_copy(
            src_ref=src, dst_ref=dst, send_sem=halo_ss.at[phase, k, n],
            recv_sem=halo_rs.at[phase, k, n], device_id=dev, device_id_type=MESH,
        )

    def halo_depth(phase, body, k):
        return [
            halo(phase, k, 0, body.at[DEP - 1, k], rim_d.at[phase, 0, k], (up_g, i)),
            halo(phase, k, 1, body.at[0, k], rim_d.at[phase, 1, k], (dn_g, i)),
        ]

    def halo_side(phase, k):
        to = up_i if k else dn_i
        side = 1 - k
        return [
            halo(phase, k, 2, edge.at[phase, k], rim_h.at[phase, side], (g, to)),
            halo(
                phase, k, 3, edge.at[phase, k, pl.ds(last, 16)],
                rim_c.at[phase, 0, side], (up_g, to),
            ),
            halo(
                phase, k, 4, edge.at[phase, k, pl.ds(0, 16)],
                rim_c.at[phase, 1, side], (dn_g, to),
            ),
        ]

    def start(copies):
        for cp in copies:
            cp.start()

    def finish(copies):
        for cp in copies:
            cp.wait()

    in_g = (g > 0, g < ng - 1)
    in_i = (i > 0, i < ni - 1)

    def part(ok, val):
        return jnp.where(ok, val.astype(F32), 0.0)

    def rim_depth(phase, k):
        for n in range(2):
            pad[(DEP + 1) * n, 1 + 2 * k : 3 + 2 * k] = part(
                in_g[n], rim_d[phase, n, k]
            ).reshape(2, WIN, WID)

    def rim_side(phase, side):
        h = (HGT + 1) * side
        for n in range(2):
            corner = part(in_g[n] & in_i[side], rim_c[phase, n, side])
            pad[(DEP + 1) * n, h] = corner[:WIN] if n else corner[WIN:]
        pad[1 : 1 + DEP, h] = part(in_i[side], rim_h[phase, side]).reshape(DEP, WIN, WID)

    def own_rows(owner):
        return pl.ds(pl.multiple_of(owner * DEP, DEP), DEP)

    high, chip, core = lax.div(g, 8), lax.rem(lax.div(g, 2), 4), lax.rem(g, 2)
    peers = []
    for step in range(ng - 1):
        far_y, far_x = step < 8, (2, 1, 3, 0)[step // 2 % 4]
        same = 1 - (step + 1) % 2
        p_y = 1 - high if far_y else high
        p_x = lax.rem(chip + far_x, 4) if far_x else chip
        p_c = core if same else 1 - core
        peers.append(p_y * 8 + p_x * 2 + p_c)

    def exchange(kind, col, src, dst):
        for p in peers:
            pltpu.make_async_remote_copy(
                src_ref=src.at[col, own_rows(p)], dst_ref=dst.at[col, own_rows(g)],
                send_sem=a2a_ss.at[kind, col], recv_sem=a2a_rs.at[kind, col],
                device_id=(p, i), device_id_type=MESH,
            ).start()
        pltpu.make_async_copy(
            src.at[col, own_rows(g)], dst.at[col, own_rows(g)], a2a_rs.at[kind, col]
        ).start()

    def arrived(kind, col, dst):
        pltpu.make_async_copy(dst.at[col], dst.at[col], a2a_rs.at[kind, col]).wait()

    def sent(kind, col, src):
        rows = pl.ds(0, LEN - DEP)
        pltpu.make_async_copy(
            src.at[col, rows], src.at[col, rows], a2a_ss.at[kind, col]
        ).wait()

    def filtered(d, h, flip):
        return conv_row(pad, taps, d, h, flip) + pad[d + 1, h + 1]

    def middle(flip, first, count):
        def one(d, carry):
            for k in range(2):
                mid[k, d] = filtered(d, 1 + k, flip)
            return carry

        lax.fori_loop(first, first + count, one, 0, unroll=2 if count > 1 else 1)

    def both_rows(d, k, flip):
        outer = filtered(d, 3 * k, flip)
        rows = [mid[k, d], outer] if k else [outer, mid[k, d]]
        return jnp.concatenate(rows, 0).astype(BF16)

    def fill(d, carry):
        pad[1 + d, 1 : 1 + HGT] = tok[d].reshape(COLS, WID).astype(F32).reshape(HGT, WIN, WID)
        return carry

    def stage(k):
        rows = tok[:, k].astype(F32).reshape(DEP, 2, WIN, WID)
        edge[0, k] = rows[:, k].reshape(DEP * WIN, WID).astype(BF16)

    loads[0].wait()
    stage(1)
    loads[1].wait()
    stage(0)
    pl.semaphore_wait(barrier, ng - 1 + len(sides))
    depth = halo_depth(0, tok, 0) + halo_depth(0, tok, 1)
    low, top = halo_side(0, 1), halo_side(0, 0)
    start(depth + low + top)
    lax.fori_loop(0, DEP, fill, 0)

    square = (LEN, LEN)
    row, lane = iota(square, 0), iota(square, 1)
    swap[...] = jnp.where(lane == (row & 15) * 16 + (row >> 4), 1.0, 0.0).astype(BF16)
    eye[...] = jnp.where(row == lane, 1.0, 0.0).astype(BF16)

    loads[3].wait()
    for k in range(2):
        send_g[k] = dot_nn(swap[...], go[:, k].reshape(LEN, WID)).astype(BF16)

    loads[2].wait()
    conv_f = conv_w[...].astype(F32)
    for n in range(27):
        taps[n] = jnp.broadcast_to(conv_f[n : n + 1], (WIN, WID))

    loads[4].wait()
    slim = (64, LEN)
    key_block = iota(slim, 0)
    query_block = iota(slim, 1) >> 6
    lower = jnp.zeros(slim, jnp.int32)
    upper = jnp.zeros(slim, jnp.int32)
    for n in range(4):
        lower = jnp.where(query_block == n, bands[0, n], lower)
        upper = jnp.where(query_block == n, bands[1, n], upper)
    banned = (key_block < query_block - lower) | (key_block > query_block + upper)
    bias[...] = jnp.where(banned & (key_block < 4), -1e30, 0.0).astype(BF16)
    wide = (LEN, 128)
    hot[...] = jnp.where((iota(wide, 1) & 63) == (iota(wide, 0) >> 6), 1.0, 0.0).astype(BF16)

    for cp in loads[5:]:
        cp.wait()
    gain_row = gain[...]

    middle(False, 1, DEP - 2)
    finish(depth)
    for k in range(2):
        rim_depth(0, k)
    middle(False, 0, 1)
    middle(False, DEP - 1, 1)

    for k in range(2):
        finish(top if k else low)
        if k == 0:
            exchange(0, 0, send_g, col_g)
        rim_side(0, k)

        def forward(d, carry, k=k):
            rows = pl.ds(pl.multiple_of(d * 16, 16), 16)
            filt[k, rows] = both_rows(d, k, False)
            return carry

        lax.fori_loop(0, DEP, forward, 0, unroll=2)
        for n in range(LEN // 64):
            rows = slice(n * 64, (n + 1) * 64)
            vals = filt[k, rows].astype(F32)
            centred = vals - jnp.sum(vals, -1, keepdims=True) * (1.0 / WID)
            var = jnp.sum(centred * centred, -1, keepdims=True) * (1.0 / WID)
            inv = lax.rsqrt(var + 1e-05)
            xhat = centred * inv
            unit[k, rows] = xhat
            scale[k, rows] = jnp.broadcast_to(inv, (64, 128))
            normed[k, rows] = (xhat * gain_row).astype(BF16)
        send_n[k] = dot_nn(swap[...], normed[k]).astype(BF16)
        exchange(1, k, send_n, col_n)

    exchange(0, 1, send_g, col_g)

    for src, dst in ((wq, wqt), (wk, wkt), (wv, wvt)):
        for n in range(2):
            half = slice(n * LEN, (n + 1) * LEN)
            dst[half] = dot_nt(eye[...], src[:, half]).astype(BF16)

    low_half = iota(wide, 1) < 64
    none = jnp.zeros(slim, BF16)
    ones = jnp.ones((16, LEN), BF16)

    def part_of(head):
        first = head // 2 * 128
        return slice(first, first + 128), slice(head * 64, head * 64 + 64)

    def attend(col):
        arrived(1, col, col_n)
        x = col_n[col]
        k_s[...] = dot_nn(x, wk[...]).astype(BF16)
        query = dot_nt(wqt[...], x).astype(BF16).astype(F32) * 0.125
        qt_s[col] = query.astype(BF16)
        vt_s[...] = dot_nt(wvt[...], x).astype(BF16)

        for head in range(8):
            lanes, feats = part_of(head)
            k2, qt = k_s[:, lanes], qt_s[col, feats]
            if head % 2 == 0:
                keys = jnp.where(low_half, k2, hot[...])
                queries = jnp.concatenate([qt, bias[...]], 0)
            else:
                keys = jnp.where(low_half, hot[...], k2)
                queries = jnp.concatenate([bias[...], qt], 0)
            scores = dot_nn(keys, queries)
            peak = jnp.max(scores, 0, keepdims=True)
            exp_s[col, head] = jnp.exp(scores - peak).astype(BF16)
        for head in range(8):
            lanes, feats = part_of(head)
            sums = dot_nn(jnp.concatenate([vt_s[feats], ones], 0), exp_s[col, head])
            inv = 1.0 / sums[64:65]
            inv_s[col, head] = jnp.broadcast_to(inv, (8, LEN))
            at_s[col, feats] = (sums[:64] * inv).astype(BF16)
        send_a[col] = at_s[col].T

    def attend_back(col):
        x = col_n[col]
        v_s[...] = dot_nn(x, wv[...]).astype(BF16)
        kt_s[...] = dot_nt(wkt[...], x).astype(BF16)
        arrived(0, col, col_g)
        gt_s[...] = dot_nt(wo[...], col_g[col]).astype(BF16)

        for head in range(8):
            lanes, feats = part_of(head)
            v2, gt_h = v_s[:, lanes], gt_s[feats]
            grads = jnp.concatenate([none, gt_h] if head % 2 else [gt_h, none], 0)
            grad_p = dot_nn(v2, grads)
            dots = at_s[col, feats].astype(F32) * gt_h.astype(F32)
            centre = jnp.sum(dots, 0, keepdims=True)
            weights = exp_s[col, head].astype(F32)
            grad_s[head] = (weights * (grad_p - centre)).astype(BF16)
        for head in range(8):
            lanes, feats = part_of(head)
            inv = inv_s[col, head][0:1]
            gt_h = (gt_s[feats].astype(F32) * inv).astype(BF16)
            gv_s[feats] = dot_nt(gt_h, exp_s[col, head]).astype(BF16)
            query = (qt_s[col, feats].astype(F32) * inv).astype(BF16)
            gk_s[feats] = dot_nt(query, grad_s[head]).astype(BF16)
            key = dot_nn(kt_s[feats], grad_s[head])
            gq_s[feats] = (key * (inv * 0.125)).astype(BF16)
        send_b[col] = (
            dot_tn(gq_s[...], wqt[...]) + dot_tn(gk_s[...], wkt[...]) + dot_tn(gv_s[...], wvt[...])
        ).astype(BF16)

    def project(k):
        arrived(3, k, ret_a)
        att = dot_nn(swap[...], ret_a[k]).astype(BF16)
        whole = filt[k].astype(F32) + dot_nn(att, wo[...])
        out[:, k] = whole.astype(BF16).reshape(DEP, 16, WID)
        cp = pltpu.make_async_copy(out.at[:, k], out_h.at[:, k], store_sem.at[0, k])
        cp.start()
        return cp

    attend(0)
    exchange(3, 0, send_a, ret_a)
    attend(1)
    exchange(3, 1, send_a, ret_a)
    attend_back(0)
    exchange(2, 0, send_b, ret_b)
    attend_back(1)
    exchange(2, 1, send_b, ret_b)
    stores = [project(0)]

    depth = []
    sides = []
    for k in range(2):
        arrived(2, k, ret_b)
        unit_grad = dot_nn(swap[...], ret_b[k]) * gain_row
        xhat = unit[k]
        mean = jnp.sum(unit_grad, -1, keepdims=True) * (1.0 / WID)
        along = jnp.sum(unit_grad * xhat, -1, keepdims=True) * (1.0 / WID)
        inv = scale[k][:, 0:1]
        rest = go[:, k].reshape(LEN, WID).astype(F32)
        rounded = (rest + inv * (unit_grad - mean - xhat * along)).astype(BF16)
        grad_f[:, k] = rounded.reshape(DEP, 16, WID)
        values = rounded.astype(F32).reshape(DEP, 2, WIN, WID)
        pad[1 : 1 + DEP, 1 + 2 * k : 3 + 2 * k] = values
        edge[1, k] = values[:, k].reshape(DEP * WIN, WID).astype(BF16)
        new = halo_side(1, k), halo_depth(1, grad_f, k)
        start(new[1] + new[0])
        sides.append(new[0])
        depth.append(new[1])

    stores.append(project(1))

    def adjoint(k, first, count):
        def one(d, carry):
            gt[d, k] = both_rows(d, k, True)
            return carry

        lax.fori_loop(first, first + count, one, 0, unroll=2 if count > 1 else 1)

    middle(True, 1, DEP - 2)
    finish(sides[0])
    rim_side(1, 1)
    adjoint(1, 1, DEP - 2)
    for k in range(2):
        finish(depth[k])
        rim_depth(1, k)
    for d in (0, DEP - 1):
        middle(True, d, 1)
        adjoint(1, d, 1)
    cp = pltpu.make_async_copy(gt.at[:, 1], grad_h.at[:, 1], store_sem.at[1, 1])
    cp.start()
    stores.append(cp)
    finish(sides[1])
    rim_side(1, 0)
    for n in range(2):
        adjoint(0, n * DEP // 2, DEP // 2)
        rows = pl.ds(n * DEP // 2, DEP // 2)
        cp = pltpu.make_async_copy(gt.at[rows, 0], grad_h.at[rows, 0], store_sem.at[2, n])
        cp.start()
        stores.append(cp)
    for kind, src in enumerate((send_g, send_n, send_b, send_a)):
        for col in range(PER):
            sent(kind, col, src)
    finish(stores)


def hand_over(out_in, grad_in, out_ref, grad_ref, held, in_sem, out_sem):
    moves = []
    for n, (src, dst) in enumerate(((out_in, out_ref), (grad_in, grad_ref))):
        for part in range(4):
            rows = pl.ds(part * DEP // 4, DEP // 4)
            moves.append((
                pltpu.make_async_copy(src.at[rows], held.at[n, rows], in_sem.at[n, part]),
                pltpu.make_async_copy(held.at[n, rows], dst.at[rows], out_sem.at[n, part]),
            ))
    for load, _ in moves:
        load.start()
    for load, store in moves:
        load.wait()
        store.start()
    for _, store in moves:
        store.wait()


def body(tokens, conv_weight, gain, bands, w_query, w_key, w_value, w_out, grad_out):
    whole = (DEP, 2, 16, WID)
    pair = (PER, LEN, WID)
    hbm = pl.BlockSpec(memory_space=pltpu.HBM)
    scratch = [
        pltpu.SMEM((2, 4), jnp.int32),
        pltpu.VMEM((27, WID), BF16),
        pltpu.VMEM((1, WID), F32),
        pltpu.VMEM(whole, BF16), pltpu.VMEM(whole, BF16),
        *[pltpu.VMEM((WID, WID), BF16) for _ in range(7)],
        pltpu.VMEM((27, WIN, WID), F32),
        pltpu.VMEM((DEP + 2, HGT + 2, WIN, WID), F32),
        pltpu.VMEM((2, 2, DEP * WIN, WID), BF16),
        pltpu.VMEM((2, 2, 2, 16, WID), BF16),
        pltpu.VMEM((2, 2, DEP * WIN, WID), BF16),
        pltpu.VMEM((2, 2, 2, 16, WID), BF16),
        *[pltpu.VMEM(pair, BF16) for _ in range(8)],
        pltpu.VMEM((LEN, LEN), BF16), pltpu.VMEM((LEN, LEN), BF16),
        pltpu.VMEM((64, LEN), BF16), pltpu.VMEM((LEN, 128), BF16),
        pltpu.VMEM(pair, BF16), pltpu.VMEM(pair, BF16),
        pltpu.VMEM(pair, F32),
        pltpu.VMEM((PER, LEN, 128), F32),
        *[pltpu.VMEM(whole, BF16) for _ in range(3)],
        *[pltpu.VMEM((LEN, WID), BF16) for _ in range(2)],
        pltpu.VMEM((PER, WID, LEN), BF16),
        *[pltpu.VMEM((WID, LEN), BF16) for _ in range(3)],
        pltpu.VMEM((PER, WID, LEN), BF16),
        *[pltpu.VMEM((WID, LEN), BF16) for _ in range(3)],
        pltpu.VMEM((PER, 8, LEN, LEN), BF16),
        pltpu.VMEM((PER, 8, 8, LEN), F32),
        pltpu.VMEM((8, LEN, LEN), BF16),
        pltpu.VMEM((2, DEP, WIN, WID), F32),
        pltpu.SemaphoreType.DMA((10,)),
        pltpu.SemaphoreType.DMA((2, 2, 5)), pltpu.SemaphoreType.DMA((2, 2, 5)),
        pltpu.SemaphoreType.DMA((4, PER)), pltpu.SemaphoreType.DMA((4, PER)),
        pltpu.SemaphoreType.DMA((3, 2)),
    ]
    made = pl.pallas_call(
        kernel,
        out_shape=(jax.ShapeDtypeStruct(whole, BF16), jax.ShapeDtypeStruct(whole, BF16)),
        in_specs=[hbm] * 9,
        out_specs=(hbm, hbm),
        scratch_shapes=scratch,
        compiler_params=pltpu.CompilerParams(
            collective_id=0, has_side_effects=True, vmem_limit_bytes=60 * 2**20
        ),
        name="sublayer",
    )(
        bands.T, conv_weight, gain.reshape(1, WID), tokens.reshape(whole),
        grad_out.reshape(whole), w_query, w_key, w_value, w_out,
    )
    out, grad = pl.pallas_call(
        hand_over,
        out_shape=(jax.ShapeDtypeStruct(whole, BF16), jax.ShapeDtypeStruct(whole, BF16)),
        in_specs=[hbm] * 2,
        out_specs=(hbm, hbm),
        scratch_shapes=[
            pltpu.VMEM((2, *whole), BF16),
            pltpu.SemaphoreType.DMA((2, 4)), pltpu.SemaphoreType.DMA((2, 4)),
        ],
        compiler_params=pltpu.CompilerParams(vmem_limit_bytes=60 * 2**20),
        name="hand_over",
    )(*made)
    return out.reshape(tokens.shape), grad.reshape(tokens.shape)


def solution(mesh):
    slab = P("grp", "inner", None, None)
    in_specs = (slab, P(), P(), P(), P(), P(), P(), P(), slab)
    return jax.shard_map(
        body, mesh=mesh, in_specs=in_specs, out_specs=(slab, slab), check_vma=False
    )
```
